1024 devices in a mesh: node: 8 (over x_lo, core), cross: 128 (over z, y, x_hi).
Axes of the slice: x: 8 (x_hi: 2, x_lo: 4; x = x_hi * 4 + x_lo), y: 8, z: 8, core: 2. Of those that a mesh axis runs over, the one named last changes fastest.
Arguments:
- grads: bfloat16 [1024, 1024, 256], P(('node', 'cross')), may hold values from -6 to 6
- master: float32 [1024, 256], P(('node', 'cross')), may hold values from -0.3125 to 0.3125
- moment: float32 [1024, 256], P(('node', 'cross')), may hold values from -4 to 4
- second: float32 [1024, 256], P(('node', 'cross')), may hold values from 0.1 to 4
Outputs:
- master_new: float32 [1024, 256], P(('node', 'cross'))
- moment_new: float32 [1024, 256], P(('node', 'cross'))
- second_new: float32 [1024, 256], P(('node', 'cross'))
- weight_values: bfloat16 [1024, 256], replicated
- weight_scales: bfloat16 [1024], replicated
The draws below stay inside these ranges and needn't reach their ends.
All inputs are finite; a program needn't handle non-finite values.
Results may differ from the reference program's by a relative error of at most 0.015.
Values may be sent and summed in bfloat16 or wider, within the bound.
No kernel may reach another device: no remote copies, remote signals or barrier semaphores. Data moves between devices by JAX's collectives and lax.ppermute only.
A program may use at most 32 MiB of HBM per device.

```python
import math
import jax
import jax.numpy as jnp
from jax import lax

BLOCK = 256
BLOCKS = 1024
N_NODE = 8
N_CROSS = 128
DEVICES = 1024


def strengthened(result, rng, source, target, blocks, factor):
    def block_of(dim):
        return (jnp.arange(result.shape[dim]) // (result.shape[dim] // blocks)).reshape((-1,) + (1,) * (result.ndim - 1 - dim))

    first = jax.random.permutation(rng, blocks)[block_of(target)]
    other_side = (block_of(target) + blocks // 2) % blocks
    return jnp.where((block_of(source) == first) | (block_of(source) == other_side), factor * result, result)


def levels(key, shape, cuts, smallest, high):
    level = 1.0
    for position, shards_of in cuts:
        heights = jax.random.uniform(jax.random.fold_in(jax.random.fold_in(key, 6), position), (shards_of,), jnp.float32, smallest / len(cuts), high / len(cuts))
        level = level * jnp.repeat(jnp.exp(heights), shape[position] // shards_of).reshape((-1,) + (1,) * (len(shape) - 1 - position))
    return level


def normal_values(stream_key, shape, width, bound, shards=(), dtype=jnp.bfloat16):
    loudness = levels(stream_key, shape, shards, -0.22, 0.18) if shards else 1.0
    array = jax.random.normal(stream_key, shape, jnp.float32) * width * loudness
    return jnp.minimum(jnp.maximum(array, -bound), bound).astype(dtype)


def noise_with(key, extent, scale, limit, cuts, heavy, kind=jnp.bfloat16):
    entries = scale * jax.random.normal(key, extent, jnp.float32)
    if cuts:
        entries = entries * levels(key, extent, cuts, -0.22, 0.18)
    return jnp.clip(strengthened(entries, jax.random.fold_in(key, 3), *heavy), -limit, limit).astype(kind)


def setup_inputs(seed: int = 0) -> dict:
    seeds = jax.random.split(jax.random.key(seed), 5)
    return {
        "grads": noise_with(seeds[0], (DEVICES, BLOCKS, BLOCK), 0.125, 6.0, ((0, 1024),), (0, 1, 1024, 6.0)),
        "master": normal_values(seeds[1], (BLOCKS, BLOCK), 0.02, 0.3125, ((0, 1024),), jnp.float32),
        "moment": normal_values(seeds[2], (BLOCKS, BLOCK), 0.3, 4.0, ((0, 1024),), jnp.float32),
        "second": jnp.clip(jnp.exp(math.log(4.0) - 3.6888794 * jax.random.uniform(seeds[3], (BLOCKS, BLOCK), jnp.float32) ** levels(seeds[3], (BLOCKS, BLOCK), ((0, 1024),), -0.2, 0.2)), 0.1, 4.0),
    }


EPS_SCALE = 1e-05
BETA_ONE = 0.9
BETA_TWO = 0.95
LEARN_RATE = 0.02
DECAY_RATE = 0.1
EPS_ADAM = 1e-08
CORRECT_ONE = 1.0 - 0.9 ** 10
CORRECT_TWO = 1.0 - 0.95 ** 10

def quantize(values):
    scales = (lax.optimization_barrier(jnp.max(jnp.abs(values), axis=-1)) + EPS_SCALE).astype(jnp.bfloat16)
    wide = lax.optimization_barrier(scales).astype(jnp.float32)
    return ((values / wide[..., None]).astype(jnp.bfloat16), scales)

def dequantize(quant, scales):
    return quant.astype(jnp.float32) * scales.astype(jnp.float32)[..., None]

def reference(grads, master, moment, second):
    grouped = grads.reshape(N_NODE, N_CROSS, BLOCKS, BLOCK)

    def section(partial_value, grad_rows):
        quant, scales = quantize(grad_rows.astype(jnp.float32))
        return (partial_value + dequantize(quant, scales), None)
    partial_value, unused = lax.scan(section, jnp.zeros((N_CROSS, BLOCKS, BLOCK), jnp.float32), grouped)
    quant_two, scale_two = quantize(partial_value)
    summed = lax.optimization_barrier(jnp.sum(dequantize(quant_two, scale_two), axis=0))
    moment_new = BETA_ONE * moment + (1.0 - BETA_ONE) * summed
    second_new = BETA_TWO * second + (1.0 - BETA_TWO) * summed * summed
    update = moment_new / CORRECT_ONE / (jnp.sqrt(second_new / CORRECT_TWO) + EPS_ADAM)
    master_new = master - LEARN_RATE * (update + DECAY_RATE * master)
    weight_values, weight_scales = quantize(master_new)
    return (master_new, moment_new, second_new, weight_values, weight_scales)
```

```python
import jax
import jax.numpy as jnp
from jax import lax
from jax.sharding import PartitionSpec as P

EPS_SCALE = 1e-05
BETA_ONE = 0.9
BETA_TWO = 0.95
LEARN_RATE = 0.02
DECAY_RATE = 0.1
EPS_ADAM = 1e-08
CORRECT_ONE = 1.0 - 0.9**10
CORRECT_TWO = 1.0 - 0.95**10


def quantize(values):
    scales = (jnp.max(jnp.abs(values), axis=-1) + EPS_SCALE).astype(jnp.bfloat16)
    wide = lax.optimization_barrier(scales).astype(jnp.float32)
    return ((values / wide[..., None]).astype(jnp.bfloat16), scales)


def exchange(rows, axis):
    return lax.all_to_all(rows, axis, split_axis=0, concat_axis=0, tiled=True)


def on_device(grads, master, moment, second):
    n_node = lax.axis_size("node")
    n_cross = lax.axis_size("cross")
    grad_rows = grads[0]
    blocks, width = grad_rows.shape
    share = blocks // n_node
    recv = exchange(grad_rows.reshape(n_node, share, width), "node")
    partial = jnp.sum(recv.astype(jnp.float32), axis=0).astype(jnp.bfloat16)
    owned = exchange(partial, "cross")
    summed = jnp.sum(owned.astype(jnp.float32), axis=0, keepdims=True)
    moment_new = BETA_ONE * moment + (1.0 - BETA_ONE) * summed
    second_new = BETA_TWO * second + (1.0 - BETA_TWO) * summed * summed
    update = moment_new / CORRECT_ONE / (jnp.sqrt(second_new / CORRECT_TWO) + EPS_ADAM)
    master_new = master - LEARN_RATE * (update + DECAY_RATE * master)
    quant, scale = quantize(master_new)
    packed = jnp.concatenate([quant, jnp.broadcast_to(scale[:, None], (1, width))], axis=1)
    shared = exchange(jnp.broadcast_to(packed, (n_cross, 2 * width)), "cross")
    scale_rows = jnp.pad(shared[:, width][None, :], ((0, 15), (0, width - n_cross)))
    rows = jnp.concatenate([shared[:, :width], scale_rows], axis=0)
    whole = lax.all_gather(rows, "node", axis=0, tiled=False)
    weight_values = whole[:, :share].reshape(blocks, width)
    weight_scales = whole[:, share, :share].reshape(blocks)
    return (master_new, moment_new, second_new, weight_values, weight_scales)


def solution(mesh):
    rows = P(("node", "cross"), None)
    return jax.shard_map(
        on_device,
        mesh=mesh,
        in_specs=(P(("node", "cross"), None, None), rows, rows, rows),
        out_specs=(rows, rows, rows, P(), P()),
        check_vma=False,
    )
```

```python
import jax
import jax.numpy as jnp
from jax import lax
from jax.experimental import pallas as pl
from jax.experimental.pallas import tpu as pltpu
from jax.sharding import Mesh
from jax.sharding import PartitionSpec as P

EPS_SCALE = 1e-05
BETA_ONE = 0.9
BETA_TWO = 0.95
LEARN_RATE = 0.02
DECAY_RATE = 0.1
EPS_ADAM = 1e-08
CORRECT_ONE = 1.0 - 0.9**10
CORRECT_TWO = 1.0 - 0.95**10

AXES = ("x_lo", "core", "z", "y", "x_hi")
SIZES = (4, 2, 8, 8, 2)
X_LO, CORE, Z, Y, X_HI = SIZES
PLANE = ("x_lo", "y", "x_hi")
Q = Y * X_HI
PEERS = X_LO * Q
WIDTH = 256
F32 = jnp.float32
BF16 = jnp.bfloat16


def pair_sum_kernel(core_ref, own_ref, got_ref, out_ref, total):
    core = core_ref[0]
    for x in range(X_LO):
        rows = pl.ds(x * Z * Q, Z * Q)
        both = own_ref[x, core].astype(F32) + got_ref[x].astype(F32)
        for half in range(2):
            total[half, rows, :] = both[:, half * 128 : half * 128 + 128]
    for x in range(X_LO):
        for q in range(Q):
            for half in range(2):
                picked = total[half, pl.ds(x * Z * Q + q, Z, stride=Q), :]
                out_ref[x * Q + q, :, half * 128 : half * 128 + 128] = picked.astype(BF16)


def plane_sum_kernel(got_ref, master_ref, moment_ref, second_ref, out_ref):
    lanes = [got_ref[p].astype(F32) for p in range(8)]
    for p in range(8, PEERS):
        lanes[p % 8] = lanes[p % 8] + got_ref[p].astype(F32)
    while len(lanes) > 1:
        lanes = [a + b for a, b in zip(lanes[::2], lanes[1::2])]
    for p in range(Z):
        out_ref[p, 0:8, :] = lanes[0]
        out_ref[p, 8:16, :] = jnp.zeros((8, WIDTH), F32)
        out_ref[p, 8:9, :] = master_ref[...]
        out_ref[p, 9:10, :] = moment_ref[...]
        out_ref[p, 10:11, :] = second_ref[...]


def update_kernel(z_ref, got_ref, out_ref, master_ref, moment_ref, second_ref):
    summed = got_ref[0, 0:8, :]
    for p in range(1, Z):
        summed = summed + got_ref[p, 0:8, :]
    master, moment, second = (
        jnp.concatenate([got_ref[p, 8 + k : 9 + k, :] for p in range(Z)], axis=0) for k in range(3)
    )
    moment_new = BETA_ONE * moment + (1.0 - BETA_ONE) * summed
    second_new = BETA_TWO * second + (1.0 - BETA_TWO) * summed * summed
    update = moment_new / CORRECT_ONE / (jnp.sqrt(second_new / CORRECT_TWO) + EPS_ADAM)
    master_new = master - LEARN_RATE * (update + DECAY_RATE * master)
    mine = lax.broadcasted_iota(jnp.int32, (Z, WIDTH), 0) == z_ref[0]
    for ref, rows in ((master_ref, master_new), (moment_ref, moment_new), (second_ref, second_new)):
        ref[...] = jnp.sum(jnp.where(mine, rows, 0.0), axis=0, keepdims=True)
    sent = master_new.astype(BF16)
    for p in range(PEERS):
        out_ref[p] = sent


def quantize_kernel(core_ref, own_ref, got_ref, values_ref, scales_ref, rows_in_order, scale_rows):
    core = core_ref[0]
    lane = lax.broadcasted_iota(jnp.int32, (Z, 128), 1)
    row = lax.broadcasted_iota(jnp.int32, (Z, 128), 0)
    for which, ref in ((core, own_ref), (1 - core, got_ref)):
        for x in range(X_LO):
            spread = jnp.zeros((Z, 128), F32)
            for q in range(Q):
                weights = ref[x * Q + q].astype(F32)
                scale = (jnp.max(jnp.abs(weights), axis=-1, keepdims=True) + EPS_SCALE).astype(BF16).astype(F32)
                values = weights / scale
                for half in range(2):
                    rows_in_order[half, pl.ds(q, Z, stride=Q), :] = values[:, half * 128 : half * 128 + 128]
                spread = jnp.where(lane % Q == q, scale, spread)
            for half in range(2):
                values_ref[x, which, :, half * 128 : half * 128 + 128] = rows_in_order[half].astype(BF16)
            scale_rows[pl.ds(x * CORE + which, 1), :] = jnp.sum(
                jnp.where(lane // Q == row, spread, 0.0), axis=0, keepdims=True
            )
    scales_ref[...] = scale_rows[...].astype(BF16)


def vmem(count):
    return [pl.BlockSpec(memory_space=pltpu.VMEM)] * count


def scalar():
    return pl.BlockSpec(memory_space=pltpu.SMEM)


def exchange(rows, axis):
    return lax.all_to_all(rows, axis, split_axis=0, concat_axis=0, tiled=True)


def swap(rows):
    return lax.ppermute(rows, "core", [(0, 1), (1, 0)])


def on_device(grads, master, moment, second):
    core = lax.axis_index("core")
    core_index = core.astype(jnp.int32)[None]
    z_index = lax.axis_index("z").astype(jnp.int32)[None]
    halves = grads.reshape(X_LO, CORE, Z * Q, WIDTH)
    other = swap(lax.dynamic_index_in_dim(halves, 1 - core, axis=1, keepdims=False))
    pair = pl.pallas_call(
        pair_sum_kernel,
        out_shape=jax.ShapeDtypeStruct((PEERS, Z, WIDTH), BF16),
        in_specs=[scalar(), *vmem(2)],
        out_specs=vmem(1)[0],
        scratch_shapes=[pltpu.VMEM((2, X_LO * Z * Q, 128), F32)],
    )(core_index, halves, other)
    column = pl.pallas_call(
        plane_sum_kernel,
        out_shape=jax.ShapeDtypeStruct((Z, 16, WIDTH), F32),
        in_specs=vmem(4),
        out_specs=vmem(1)[0],
    )(exchange(pair, PLANE), master, moment, second)
    state = jax.ShapeDtypeStruct((1, WIDTH), F32)
    weights, master_new, moment_new, second_new = pl.pallas_call(
        update_kernel,
        out_shape=(jax.ShapeDtypeStruct((PEERS, Z, WIDTH), BF16), state, state, state),
        in_specs=[scalar(), *vmem(1)],
        out_specs=vmem(4),
    )(z_index, exchange(column, "z"))
    gathered = exchange(weights, PLANE)
    values, scales = pl.pallas_call(
        quantize_kernel,
        out_shape=(
            jax.ShapeDtypeStruct((X_LO, CORE, Z * Q, WIDTH), BF16),
            jax.ShapeDtypeStruct((X_LO * CORE, Z * Q), BF16),
        ),
        in_specs=[scalar(), *vmem(2)],
        out_specs=vmem(2),
        scratch_shapes=[pltpu.VMEM((2, Z * Q, 128), F32), pltpu.VMEM((X_LO * CORE, Z * Q), F32)],
    )(core_index, gathered, swap(gathered))
    return (master_new, moment_new, second_new, values.reshape(-1, WIDTH), scales.reshape(-1))


def solution(mesh):
    devices = Mesh(mesh.devices.reshape(SIZES), AXES)
    rows = P(AXES, None)
    return jax.shard_map(
        on_device,
        mesh=devices,
        in_specs=(P(AXES, None, None), rows, rows, rows),
        out_specs=(rows, rows, rows, P(), P()),
        check_vma=False,
    )
```

```python
import jax
import jax.numpy as jnp
from jax import lax
from jax.experimental import pallas as pl
from jax.experimental.pallas import tpu as pltpu
from jax.sharding import Mesh
from jax.sharding import PartitionSpec as P

EPS_SCALE = 1e-05
BETA_ONE = 0.9
BETA_TWO = 0.95
LEARN_RATE = 0.02
DECAY_RATE = 0.1
EPS_ADAM = 1e-08
CORRECT_ONE = 1.0 - 0.9**10
CORRECT_TWO = 1.0 - 0.95**10

AXES = ("x_lo", "core", "z", "y", "x_hi")
SIZES = (4, 2, 8, 8, 2)
X_LO, CORE, Z, Y, X_HI = SIZES
PLANE = ("x_lo", "y", "x_hi")
Q = Y * X_HI
PEERS = X_LO * Q
WIDTH = 256
F32 = jnp.float32
BF16 = jnp.bfloat16
SMALL = pltpu.CompilerParams(vmem_limit_bytes=8 * 2**20)


def pair_sum_kernel(core_ref, own_ref, got_ref, out_ref, total):
    core = core_ref[0]
    for x in range(X_LO):
        rows = pl.ds(x * Z * Q, Z * Q)
        both = own_ref[x, core].astype(F32) + got_ref[x].astype(F32)
        for half in range(2):
            total[half, rows, :] = both[:, half * 128 : half * 128 + 128]
    for x in range(X_LO):
        for q in range(Q):
            for half in range(2):
                picked = total[half, pl.ds(x * Z * Q + q, Z, stride=Q), :]
                out_ref[x * Q + q, :, half * 128 : half * 128 + 128] = picked.astype(BF16)


def pieces(values, count):
    parts = []
    for _ in range(count):
        parts.append(values.astype(BF16).astype(F32))
        values = values - parts[-1]
    return parts


def plane_sum_kernel(got_ref, master_ref, moment_ref, second_ref, out_ref):
    lanes = [got_ref[p].astype(F32) for p in range(8)]
    for p in range(8, PEERS):
        lanes[p % 8] = lanes[p % 8] + got_ref[p].astype(F32)
    while len(lanes) > 1:
        lanes = [a + b for a, b in zip(lanes[::2], lanes[1::2])]
    parts = [*pieces(master_ref[...], 3), *pieces(moment_ref[...], 2), *pieces(second_ref[...], 2)]
    parts.append(jnp.zeros((1, WIDTH), F32))
    rows = jnp.concatenate([lanes[0], *parts], axis=0).astype(BF16)
    for p in range(Z):
        out_ref[p] = rows


def adamw(master, moment, second, summed):
    moment_new = BETA_ONE * moment + (1.0 - BETA_ONE) * summed
    second_new = BETA_TWO * second + (1.0 - BETA_TWO) * summed * summed
    update = moment_new / CORRECT_ONE / (jnp.sqrt(second_new / CORRECT_TWO) + EPS_ADAM)
    return master - LEARN_RATE * (update + DECAY_RATE * master), moment_new, second_new


def update_kernel(z_ref, got_ref, master_in, moment_in, second_in, out_ref, master_ref, moment_ref, second_ref):
    got = [got_ref[p].astype(F32) for p in range(Z)]
    summed = got[0][0:8]
    for p in range(1, Z):
        summed = summed + got[p][0:8]
    row = lax.broadcasted_iota(jnp.int32, (Z, WIDTH), 0)

    def state(first, count):
        rows = jnp.zeros((Z, WIDTH), F32)
        for p in range(Z):
            value = got[p][first : first + 1]
            for k in range(1, count):
                value = value + got[p][first + k : first + k + 1]
            rows = jnp.where(row == p, value, rows)
        return rows

    sent = adamw(state(8, 3), state(11, 2), state(13, 2), summed)[0].astype(BF16)
    for p in range(PEERS):
        out_ref[p] = sent
    mine = jnp.sum(jnp.where(row == z_ref[0], summed, 0.0), axis=0, keepdims=True)
    own = adamw(master_in[...], moment_in[...], second_in[...], mine)
    master_ref[...], moment_ref[...], second_ref[...] = own


def quantize_kernel(core_ref, own_ref, got_ref, values_ref, scales_ref, rows_in_order, scale_rows):
    core = core_ref[0]
    lane = lax.broadcasted_iota(jnp.int32, (Z, 128), 1)
    row = lax.broadcasted_iota(jnp.int32, (Z, 128), 0)
    for which, ref in ((core, own_ref), (1 - core, got_ref)):
        for x in range(X_LO):
            spread = jnp.zeros((Z, 128), F32)
            for q in range(Q):
                weights = ref[x * Q + q].astype(F32)
                scale = (jnp.max(jnp.abs(weights), axis=-1, keepdims=True) + EPS_SCALE).astype(BF16).astype(F32)
                values = weights / scale
                for half in range(2):
                    rows_in_order[half, pl.ds(q, Z, stride=Q), :] = values[:, half * 128 : half * 128 + 128]
                spread = jnp.where(lane % Q == q, scale, spread)
            for half in range(2):
                values_ref[x, which, :, half * 128 : half * 128 + 128] = rows_in_order[half].astype(BF16)
            scale_rows[pl.ds(x * CORE + which, 1), :] = jnp.sum(
                jnp.where(lane // Q == row, spread, 0.0), axis=0, keepdims=True
            )
    scales_ref[...] = scale_rows[...].astype(BF16)


def vmem(count):
    return [pl.BlockSpec(memory_space=pltpu.VMEM)] * count


def scalar():
    return pl.BlockSpec(memory_space=pltpu.SMEM)


def exchange(rows, axis):
    return lax.all_to_all(rows, axis, split_axis=0, concat_axis=0, tiled=True)


def swap(rows):
    return lax.ppermute(rows, "core", [(0, 1), (1, 0)])


def on_device(grads, master, moment, second):
    core = lax.axis_index("core")
    core_index = core.astype(jnp.int32)[None]
    z_index = lax.axis_index("z").astype(jnp.int32)[None]
    halves = grads.reshape(X_LO, CORE, Z * Q, WIDTH)
    other = swap(lax.dynamic_index_in_dim(halves, 1 - core, axis=1, keepdims=False))
    pair = pl.pallas_call(
        pair_sum_kernel,
        out_shape=jax.ShapeDtypeStruct((PEERS, Z, WIDTH), BF16),
        in_specs=[scalar(), *vmem(2)],
        out_specs=vmem(1)[0],
        scratch_shapes=[pltpu.VMEM((2, X_LO * Z * Q, 128), F32)],
        compiler_params=SMALL,
    )(core_index, halves, other)
    column = pl.pallas_call(
        plane_sum_kernel,
        out_shape=jax.ShapeDtypeStruct((Z, 16, WIDTH), BF16),
        in_specs=vmem(4),
        out_specs=vmem(1)[0],
        compiler_params=SMALL,
    )(exchange(pair, PLANE), master, moment, second)
    state = jax.ShapeDtypeStruct((1, WIDTH), F32)
    weights, master_new, moment_new, second_new = pl.pallas_call(
        update_kernel,
        out_shape=(jax.ShapeDtypeStruct((PEERS, Z, WIDTH), BF16), state, state, state),
        in_specs=[scalar(), *vmem(4)],
        out_specs=vmem(4),
        compiler_params=SMALL,
    )(z_index, exchange(column, "z"), master, moment, second)
    gathered = exchange(weights, PLANE)
    values, scales = pl.pallas_call(
        quantize_kernel,
        out_shape=(
            jax.ShapeDtypeStruct((X_LO, CORE, Z * Q, WIDTH), BF16),
            jax.ShapeDtypeStruct((X_LO * CORE, Z * Q), BF16),
        ),
        in_specs=[scalar(), *vmem(2)],
        out_specs=vmem(2),
        scratch_shapes=[pltpu.VMEM((2, Z * Q, 128), F32), pltpu.VMEM((X_LO * CORE, Z * Q), F32)],
        compiler_params=SMALL,
    )(core_index, gathered, swap(gathered))
    return (master_new, moment_new, second_new, values.reshape(-1, WIDTH), scales.reshape(-1))


def solution(mesh):
    devices = Mesh(mesh.devices.reshape(SIZES), AXES)
    rows = P(AXES, None)
    return jax.shard_map(
        on_device,
        mesh=devices,
        in_specs=(P(AXES, None, None), rows, rows, rows),
        out_specs=(rows, rows, rows, P(), P()),
        check_vma=False,
    )
```

```python
import jax
import jax.numpy as jnp
from jax import lax
from jax.experimental import pallas as pl
from jax.experimental.pallas import tpu as pltpu
from jax.sharding import Mesh
from jax.sharding import PartitionSpec as P

EPS_SCALE = 1e-05
BETA_ONE = 0.9
BETA_TWO = 0.95
LEARN_RATE = 0.02
DECAY_RATE = 0.1
EPS_ADAM = 1e-08
CORRECT_ONE = 1.0 - 0.9**10
CORRECT_TWO = 1.0 - 0.95**10

AXES = ("x_lo", "core", "z", "y", "x_hi")
SIZES = (4, 2, 8, 8, 2)
X_LO, CORE, Z, Y, X_HI = SIZES
PLANE = ("x_lo", "y", "x_hi")
Q = Y * X_HI
PEERS = X_LO * Q
WIDTH = 256
F32 = jnp.float32
BF16 = jnp.bfloat16
SMALL = pltpu.CompilerParams(vmem_limit_bytes=8 * 2**20)


def pair_sum_kernel(core_ref, own_ref, got_ref, out_ref, total):
    core = core_ref[0]
    for x in range(X_LO):
        rows = pl.ds(x * Z * Q, Z * Q)
        both = own_ref[x, core].astype(F32) + got_ref[x, core].astype(F32)
        for half in range(2):
            total[half, rows, :] = both[:, half * 128 : half * 128 + 128]
    for x in range(X_LO):
        for q in range(Q):
            for half in range(2):
                picked = total[half, pl.ds(x * Z * Q + q, Z, stride=Q), :]
                out_ref[x * Q + q, :, half * 128 : half * 128 + 128] = picked.astype(BF16)


def pieces(values, count):
    parts = []
    for _ in range(count):
        parts.append(values.astype(BF16).astype(F32))
        values = values - parts[-1]
    return parts


def plane_sum_kernel(got_ref, master_ref, moment_ref, second_ref, out_ref):
    lanes = [got_ref[p].astype(F32) for p in range(8)]
    for p in range(8, PEERS):
        lanes[p % 8] = lanes[p % 8] + got_ref[p].astype(F32)
    while len(lanes) > 1:
        lanes = [a + b for a, b in zip(lanes[::2], lanes[1::2])]
    parts = [*pieces(master_ref[...], 3), *pieces(moment_ref[...], 2), *pieces(second_ref[...], 2)]
    parts.append(jnp.zeros((1, WIDTH), F32))
    rows = jnp.concatenate([lanes[0], *parts], axis=0).astype(BF16)
    for p in range(Z):
        out_ref[p] = rows


def adamw(master, moment, second, summed):
    moment_new = BETA_ONE * moment + (1.0 - BETA_ONE) * summed
    second_new = BETA_TWO * second + (1.0 - BETA_TWO) * summed * summed
    update = moment_new / CORRECT_ONE / (jnp.sqrt(second_new / CORRECT_TWO) + EPS_ADAM)
    return master - LEARN_RATE * (update + DECAY_RATE * master), moment_new, second_new


def update_kernel(z_ref, got_ref, master_in, moment_in, second_in, out_ref, master_ref, moment_ref, second_ref):
    got = [got_ref[p].astype(F32) for p in range(Z)]
    summed = got[0][0:8]
    for p in range(1, Z):
        summed = summed + got[p][0:8]
    row = lax.broadcasted_iota(jnp.int32, (Z, WIDTH), 0)

    def state(first, count):
        rows = jnp.zeros((Z, WIDTH), F32)
        for p in range(Z):
            value = got[p][first : first + 1]
            for k in range(1, count):
                value = value + got[p][first + k : first + k + 1]
            rows = jnp.where(row == p, value, rows)
        return rows

    sent = adamw(state(8, 3), state(11, 2), state(13, 2), summed)[0].astype(BF16)
    for p in range(PEERS):
        out_ref[p] = sent
    mine = jnp.sum(jnp.where(row == z_ref[0], summed, 0.0), axis=0, keepdims=True)
    own = adamw(master_in[...], moment_in[...], second_in[...], mine)
    master_ref[...], moment_ref[...], second_ref[...] = own


def quantize_half(ref, write, rows_in_order):
    lane = lax.broadcasted_iota(jnp.int32, (Z, 128), 1)
    row = lax.broadcasted_iota(jnp.int32, (Z, 128), 0)
    for x in range(X_LO):
        spread = jnp.zeros((Z, 128), F32)
        for q in range(Q):
            weights = ref[x * Q + q].astype(F32)
            scale = (jnp.max(jnp.abs(weights), axis=-1, keepdims=True) + EPS_SCALE).astype(BF16).astype(F32)
            values = weights / scale
            for half in range(2):
                rows_in_order[half, pl.ds(q, Z, stride=Q), :] = values[:, half * 128 : half * 128 + 128]
            spread = jnp.where(lane % Q == q, scale, spread)
        write(x, jnp.sum(jnp.where(lane // Q == row, spread, 0.0), axis=0, keepdims=True))


def quantize_own_kernel(own_ref, values_ref, scales_ref, rows_in_order):
    def write(x, scales):
        for half in range(2):
            values_ref[x, :, half * 128 : half * 128 + 128] = rows_in_order[half].astype(BF16)
        scales_ref[x : x + 1, :] = scales

    quantize_half(own_ref, write, rows_in_order)


def quantize_all_kernel(core_ref, own_values_ref, own_scales_ref, got_ref, values_ref, scales_ref, rows_in_order, scale_rows):
    core = core_ref[0]
    for x in range(X_LO):
        values_ref[x, core] = own_values_ref[x]
        scale_rows[pl.ds(x * CORE + core, 1), :] = own_scales_ref[x : x + 1, :]

    def write(x, scales):
        for half in range(2):
            values_ref[x, 1 - core, :, half * 128 : half * 128 + 128] = rows_in_order[half].astype(BF16)
        scale_rows[pl.ds(x * CORE + 1 - core, 1), :] = scales

    quantize_half(got_ref, write, rows_in_order)
    scales_ref[...] = scale_rows[...].astype(BF16)


def vmem(count):
    return [pl.BlockSpec(memory_space=pltpu.VMEM)] * count


def scalar():
    return pl.BlockSpec(memory_space=pltpu.SMEM)


def exchange(rows, axis):
    return lax.all_to_all(rows, axis, split_axis=0, concat_axis=0, tiled=True)


def swap(rows):
    return lax.ppermute(rows, "core", [(0, 1), (1, 0)])


def on_device(grads, master, moment, second):
    core = lax.axis_index("core")
    core_index = core.astype(jnp.int32)[None]
    z_index = lax.axis_index("z").astype(jnp.int32)[None]
    halves = grads.reshape(X_LO, CORE, Z * Q, WIDTH)
    other = swap(halves)
    pair = pl.pallas_call(
        pair_sum_kernel,
        out_shape=jax.ShapeDtypeStruct((PEERS, Z, WIDTH), BF16),
        in_specs=[scalar(), *vmem(2)],
        out_specs=vmem(1)[0],
        scratch_shapes=[pltpu.VMEM((2, X_LO * Z * Q, 128), F32)],
        compiler_params=SMALL,
    )(core_index, halves, other)
    column = pl.pallas_call(
        plane_sum_kernel,
        out_shape=jax.ShapeDtypeStruct((Z, 16, WIDTH), BF16),
        in_specs=vmem(4),
        out_specs=vmem(1)[0],
        compiler_params=SMALL,
    )(exchange(pair, PLANE), master, moment, second)
    state = jax.ShapeDtypeStruct((1, WIDTH), F32)
    weights, master_new, moment_new, second_new = pl.pallas_call(
        update_kernel,
        out_shape=(jax.ShapeDtypeStruct((PEERS, Z, WIDTH), BF16), state, state, state),
        in_specs=[scalar(), *vmem(4)],
        out_specs=vmem(4),
        compiler_params=SMALL,
    )(z_index, exchange(column, "z"), master, moment, second)
    gathered = exchange(weights, PLANE)
    in_order = pltpu.VMEM((2, Z * Q, 128), F32)
    own_values, own_scales = pl.pallas_call(
        quantize_own_kernel,
        out_shape=(
            jax.ShapeDtypeStruct((X_LO, Z * Q, WIDTH), BF16),
            jax.ShapeDtypeStruct((X_LO, Z * Q), F32),
        ),
        in_specs=vmem(1),
        out_specs=vmem(2),
        scratch_shapes=[in_order],
        compiler_params=SMALL,
        cost_estimate=pl.CostEstimate(flops=400_000, bytes_accessed=2**20, transcendentals=0),
    )(gathered)
    values, scales = pl.pallas_call(
        quantize_all_kernel,
        out_shape=(
            jax.ShapeDtypeStruct((X_LO, CORE, Z * Q, WIDTH), BF16),
            jax.ShapeDtypeStruct((X_LO * CORE, Z * Q), BF16),
        ),
        in_specs=[scalar(), *vmem(3)],
        out_specs=vmem(2),
        scratch_shapes=[in_order, pltpu.VMEM((X_LO * CORE, Z * Q), F32)],
        compiler_params=SMALL,
    )(core_index, own_values, own_scales, swap(gathered))
    return (master_new, moment_new, second_new, values.reshape(-1, WIDTH), scales.reshape(-1))


def solution(mesh):
    devices = Mesh(mesh.devices.reshape(SIZES), AXES)
    rows = P(AXES, None)
    return jax.shard_map(
        on_device,
        mesh=devices,
        in_specs=(P(AXES, None, None), rows, rows, rows),
        out_specs=(rows, rows, rows, P(), P()),
        check_vma=False,
    )
```

```python
import jax
import jax.numpy as jnp
from jax import lax
from jax.experimental import pallas as pl
from jax.experimental.pallas import tpu as pltpu
from jax.sharding import Mesh
from jax.sharding import PartitionSpec as P

EPS_SCALE = 1e-05
BETA_ONE = 0.9
BETA_TWO = 0.95
LEARN_RATE = 0.02
DECAY_RATE = 0.1
EPS_ADAM = 1e-08
CORRECT_ONE = 1.0 - 0.9**10
CORRECT_TWO = 1.0 - 0.95**10

AXES = ("x_lo", "core", "z", "y", "x_hi")
SIZES = (4, 2, 8, 8, 2)
X_LO, CORE, Z, Y, X_HI = SIZES
PLANE = ("y", "x_hi", "x_lo")
Q = Y * X_HI
PEERS = X_LO * Q
WIDTH = 256
F32 = jnp.float32
BF16 = jnp.bfloat16
SMALL = pltpu.CompilerParams(vmem_limit_bytes=8 * 2**20)


def pair_sum_kernel(core_ref, own_ref, got_ref, out_ref, total):
    core = core_ref[0]
    for x in range(X_LO):
        rows = pl.ds(x * Z * Q, Z * Q)
        both = own_ref[x].astype(F32) + got_ref[x, core].astype(F32)
        for half in range(2):
            total[half, rows, :] = both[:, half * 128 : half * 128 + 128]
    for x in range(X_LO):
        for q in range(Q):
            for half in range(2):
                picked = total[half, pl.ds(x * Z * Q + q, Z, stride=Q), :]
                out_ref[q * X_LO + x, :, half * 128 : half * 128 + 128] = picked.astype(BF16)


def pieces(values, count):
    parts = []
    for _ in range(count):
        parts.append(values.astype(BF16).astype(F32))
        values = values - parts[-1]
    return parts


def plane_sum_kernel(got_ref, master_ref, moment_ref, second_ref, out_ref):
    lanes = [got_ref[p].astype(F32) for p in range(8)]
    for p in range(8, PEERS):
        lanes[p % 8] = lanes[p % 8] + got_ref[p].astype(F32)
    while len(lanes) > 1:
        lanes = [a + b for a, b in zip(lanes[::2], lanes[1::2])]
    parts = [*pieces(master_ref[...], 3), *pieces(moment_ref[...], 2), *pieces(second_ref[...], 2)]
    parts.append(jnp.zeros((1, WIDTH), F32))
    rows = jnp.concatenate([lanes[0], *parts], axis=0).astype(BF16)
    for p in range(Z):
        out_ref[p] = rows


def adamw(master, moment, second, summed):
    moment_new = BETA_ONE * moment + (1.0 - BETA_ONE) * summed
    second_new = BETA_TWO * second + (1.0 - BETA_TWO) * summed * summed
    update = moment_new / CORRECT_ONE / (jnp.sqrt(second_new / CORRECT_TWO) + EPS_ADAM)
    return master - LEARN_RATE * (update + DECAY_RATE * master), moment_new, second_new


def update_kernel(z_ref, got_ref, master_in, moment_in, second_in, out_ref, master_ref, moment_ref, second_ref):
    got = [got_ref[p].astype(F32) for p in range(Z)]
    summed = got[0][0:8]
    for p in range(1, Z):
        summed = summed + got[p][0:8]
    row = lax.broadcasted_iota(jnp.int32, (Z, WIDTH), 0)

    def state(first, count):
        rows = jnp.zeros((Z, WIDTH), F32)
        for p in range(Z):
            value = got[p][first : first + 1]
            for k in range(1, count):
                value = value + got[p][first + k : first + k + 1]
            rows = jnp.where(row == p, value, rows)
        return rows

    sent = adamw(state(8, 3), state(11, 2), state(13, 2), summed)[0].astype(BF16)
    for p in range(PEERS):
        out_ref[p] = sent
    mine = jnp.sum(jnp.where(row == z_ref[0], summed, 0.0), axis=0, keepdims=True)
    own = adamw(master_in[...], moment_in[...], second_in[...], mine)
    master_ref[...], moment_ref[...], second_ref[...] = own


def quantize_half(ref, write, rows_in_order):
    lane = lax.broadcasted_iota(jnp.int32, (Z, 128), 1)
    row = lax.broadcasted_iota(jnp.int32, (Z, 128), 0)
    for x in range(X_LO):
        spread = jnp.zeros((Z, 128), F32)
        for q in range(Q):
            weights = ref[q * X_LO + x].astype(F32)
            scale = (jnp.max(jnp.abs(weights), axis=-1, keepdims=True) + EPS_SCALE).astype(BF16).astype(F32)
            values = weights / scale
            for half in range(2):
                rows_in_order[half, pl.ds(q, Z, stride=Q), :] = values[:, half * 128 : half * 128 + 128]
            spread = jnp.where(lane % Q == q, scale, spread)
        write(x, jnp.sum(jnp.where(lane // Q == row, spread, 0.0), axis=0, keepdims=True))


def quantize_own_kernel(own_ref, values_ref, scales_ref, rows_in_order):
    def write(x, scales):
        for half in range(2):
            values_ref[x, :, half * 128 : half * 128 + 128] = rows_in_order[half].astype(BF16)
        scales_ref[x : x + 1, :] = scales

    quantize_half(own_ref, write, rows_in_order)


def quantize_all_kernel(core_ref, own_values_ref, own_scales_ref, got_ref, values_ref, scales_ref, rows_in_order, scale_rows):
    core = core_ref[0]
    for x in range(X_LO):
        values_ref[x, core] = own_values_ref[x]
        scale_rows[pl.ds(x * CORE + core, 1), :] = own_scales_ref[x : x + 1, :]

    def write(x, scales):
        for half in range(2):
            values_ref[x, 1 - core, :, half * 128 : half * 128 + 128] = rows_in_order[half].astype(BF16)
        scale_rows[pl.ds(x * CORE + 1 - core, 1), :] = scales

    quantize_half(got_ref, write, rows_in_order)
    scales_ref[...] = scale_rows[...].astype(BF16)


def vmem(count):
    return [pl.BlockSpec(memory_space=pltpu.VMEM)] * count


def scalar():
    return pl.BlockSpec(memory_space=pltpu.SMEM)


def exchange(rows, axis):
    return lax.all_to_all(rows, axis, split_axis=0, concat_axis=0, tiled=True)


def swap(rows):
    return lax.ppermute(rows, "core", [(0, 1), (1, 0)])


def on_device(grads, master, moment, second):
    core = lax.axis_index("core")
    core_index = core.astype(jnp.int32)[None]
    z_index = lax.axis_index("z").astype(jnp.int32)[None]
    halves = grads.reshape(X_LO, CORE, Z * Q, WIDTH)
    other = swap(halves)
    own = lax.dynamic_index_in_dim(halves, core, axis=1, keepdims=False)
    pair = pl.pallas_call(
        pair_sum_kernel,
        out_shape=jax.ShapeDtypeStruct((PEERS, Z, WIDTH), BF16),
        in_specs=[scalar(), *vmem(2)],
        out_specs=vmem(1)[0],
        scratch_shapes=[pltpu.VMEM((2, X_LO * Z * Q, 128), F32)],
        compiler_params=SMALL,
    )(core_index, own, other)
    column = pl.pallas_call(
        plane_sum_kernel,
        out_shape=jax.ShapeDtypeStruct((Z, 16, WIDTH), BF16),
        in_specs=vmem(4),
        out_specs=vmem(1)[0],
        compiler_params=SMALL,
    )(exchange(pair, PLANE), master, moment, second)
    state = jax.ShapeDtypeStruct((1, WIDTH), F32)
    weights, master_new, moment_new, second_new = pl.pallas_call(
        update_kernel,
        out_shape=(jax.ShapeDtypeStruct((PEERS, Z, WIDTH), BF16), state, state, state),
        in_specs=[scalar(), *vmem(4)],
        out_specs=vmem(4),
        compiler_params=SMALL,
    )(z_index, exchange(column, "z"), master, moment, second)
    gathered = exchange(weights, PLANE)
    in_order = pltpu.VMEM((2, Z * Q, 128), F32)
    own_values, own_scales = pl.pallas_call(
        quantize_own_kernel,
        out_shape=(
            jax.ShapeDtypeStruct((X_LO, Z * Q, WIDTH), BF16),
            jax.ShapeDtypeStruct((X_LO, Z * Q), F32),
        ),
        in_specs=vmem(1),
        out_specs=vmem(2),
        scratch_shapes=[in_order],
        compiler_params=SMALL,
        cost_estimate=pl.CostEstimate(flops=400_000, bytes_accessed=2**20, transcendentals=0),
    )(gathered)
    values, scales = pl.pallas_call(
        quantize_all_kernel,
        out_shape=(
            jax.ShapeDtypeStruct((X_LO, CORE, Z * Q, WIDTH), BF16),
            jax.ShapeDtypeStruct((X_LO * CORE, Z * Q), BF16),
        ),
        in_specs=[scalar(), *vmem(3)],
        out_specs=vmem(2),
        scratch_shapes=[in_order, pltpu.VMEM((X_LO * CORE, Z * Q), F32)],
        compiler_params=SMALL,
    )(core_index, own_values, own_scales, swap(gathered))
    return (master_new, moment_new, second_new, values.reshape(-1, WIDTH), scales.reshape(-1))


def solution(mesh):
    devices = Mesh(mesh.devices.reshape(SIZES), AXES)
    rows = P(AXES, None)
    return jax.shard_map(
        on_device,
        mesh=devices,
        in_specs=(P(AXES, None, None), rows, rows, rows),
        out_specs=(rows, rows, rows, P(), P()),
        check_vma=False,
    )
```

```python
import jax
import jax.numpy as jnp
from jax import lax
from jax.experimental import pallas as pl
from jax.experimental.pallas import tpu as pltpu
from jax.sharding import Mesh
from jax.sharding import PartitionSpec as P

EPS_SCALE = 1e-05
BETA_ONE = 0.9
BETA_TWO = 0.95
LEARN_RATE = 0.02
DECAY_RATE = 0.1
EPS_ADAM = 1e-08
CORRECT_ONE = 1.0 - 0.9**10
CORRECT_TWO = 1.0 - 0.95**10

AXES = ("x_lo", "core", "z", "y", "x_hi")
SIZES = (4, 2, 8, 8, 2)
X_LO, CORE, Z, Y, X_HI = SIZES
PLANE = ("y", "x_hi", "x_lo")
Q = Y * X_HI
PEERS = X_LO * Q
WIDTH = 256
F32 = jnp.float32
BF16 = jnp.bfloat16
SMALL = pltpu.CompilerParams(vmem_limit_bytes=8 * 2**20)


def pair_sum_kernel(place_ref, own_ref, got_ref, out_ref, total):
    core = place_ref[0]
    for x in range(X_LO):
        rows = pl.ds(x * Z * Q, Z * Q)
        both = own_ref[x].astype(F32) + got_ref[x, core].astype(F32)
        for half in range(2):
            total[half, rows, :] = both[:, half * 128 : half * 128 + 128]
    for x in range(X_LO):
        for q in range(Q):
            for half in range(2):
                picked = total[half, pl.ds(x * Z * Q + q, Z, stride=Q), :]
                out_ref[q * X_LO + x, :, half * 128 : half * 128 + 128] = picked.astype(BF16)


def pieces(values, count):
    parts = []
    for _ in range(count):
        parts.append(values.astype(BF16).astype(F32))
        values = values - parts[-1]
    return parts


def plane_sum_kernel(got_ref, master_ref, moment_ref, second_ref, out_ref):
    lanes = [got_ref[p].astype(F32) for p in range(8)]
    for p in range(8, PEERS):
        lanes[p % 8] = lanes[p % 8] + got_ref[p].astype(F32)
    while len(lanes) > 1:
        lanes = [a + b for a, b in zip(lanes[::2], lanes[1::2])]
    parts = [*pieces(master_ref[...], 3), *pieces(moment_ref[...], 2), *pieces(second_ref[...], 2)]
    parts.append(jnp.zeros((1, WIDTH), F32))
    rows = jnp.concatenate([lanes[0], *parts], axis=0).astype(BF16)
    for p in range(Z):
        out_ref[p] = rows


def adamw(master, moment, second, summed):
    moment_new = BETA_ONE * moment + (1.0 - BETA_ONE) * summed
    second_new = BETA_TWO * second + (1.0 - BETA_TWO) * summed * summed
    update = moment_new / CORRECT_ONE / (jnp.sqrt(second_new / CORRECT_TWO) + EPS_ADAM)
    return master - LEARN_RATE * (update + DECAY_RATE * master), moment_new, second_new


def update_kernel(place_ref, got_ref, out_ref, mine_ref):
    got = [got_ref[p].astype(F32) for p in range(Z)]
    summed = got[0][0:8]
    for p in range(1, Z):
        summed = summed + got[p][0:8]
    row = lax.broadcasted_iota(jnp.int32, (Z, WIDTH), 0)

    def state(first, count):
        rows = jnp.zeros((Z, WIDTH), F32)
        for p in range(Z):
            value = got[p][first : first + 1]
            for k in range(1, count):
                value = value + got[p][first + k : first + k + 1]
            rows = jnp.where(row == p, value, rows)
        return rows

    sent = adamw(state(8, 3), state(11, 2), state(13, 2), summed)[0].astype(BF16)
    for p in range(PEERS):
        out_ref[p] = sent
    mine_ref[...] = jnp.sum(jnp.where(row == place_ref[1], summed, 0.0), axis=0, keepdims=True)


def quantize_half(ref, values_ref, to_core, keep_scales, rows_in_order, staged, sems):
    lane = lax.broadcasted_iota(jnp.int32, (Z, 128), 1)
    row = lax.broadcasted_iota(jnp.int32, (Z, 128), 0)
    copies = []
    for x in range(X_LO):
        spread = jnp.zeros((Z, 128), F32)
        for q in range(Q):
            weights = ref[q * X_LO + x].astype(F32)
            scale = (jnp.max(jnp.abs(weights), axis=-1, keepdims=True) + EPS_SCALE).astype(BF16).astype(F32)
            values = weights / scale
            for half in range(2):
                rows_in_order[half, pl.ds(q, Z, stride=Q), :] = values[:, half * 128 : half * 128 + 128]
            spread = jnp.where(lane % Q == q, scale, spread)
        keep_scales(x, jnp.sum(jnp.where(lane // Q == row, spread, 0.0), axis=0, keepdims=True))
        for half in range(2):
            staged[x, :, half * 128 : half * 128 + 128] = rows_in_order[half].astype(BF16)
        copies.append(pltpu.make_async_copy(staged.at[x], values_ref.at[x, to_core], sems.at[x]))
        copies[-1].start()
    return copies


def own_half_kernel(
    place_ref, own_ref, mine_ref, master_in, moment_in, second_in,
    values_ref, scales_ref, master_ref, moment_ref, second_ref, rows_in_order, staged, sems,
):
    def keep(x, scales):
        scales_ref[x : x + 1, :] = scales

    copies = quantize_half(own_ref, values_ref, place_ref[0], keep, rows_in_order, staged, sems)
    own = adamw(master_in[...], moment_in[...], second_in[...], mine_ref[...])
    master_ref[...], moment_ref[...], second_ref[...] = own
    for copy in copies:
        copy.wait()


def other_half_kernel(
    place_ref, own_scales_ref, got_ref, values_in, values_ref, scales_ref, rows_in_order, staged, scale_rows, sems
):
    core = place_ref[0]
    for x in range(X_LO):
        scale_rows[pl.ds(x * CORE + core, 1), :] = own_scales_ref[x : x + 1, :]

    def keep(x, scales):
        scale_rows[pl.ds(x * CORE + 1 - core, 1), :] = scales

    copies = quantize_half(got_ref, values_ref, 1 - core, keep, rows_in_order, staged, sems)
    scales_ref[...] = scale_rows[...].astype(BF16)
    for copy in copies:
        copy.wait()


def vmem(count):
    return [pl.BlockSpec(memory_space=pltpu.VMEM)] * count


def scalar():
    return pl.BlockSpec(memory_space=pltpu.SMEM)


def exchange(rows, axis):
    return lax.all_to_all(rows, axis, split_axis=0, concat_axis=0, tiled=True)


def swap(rows):
    return lax.ppermute(rows, "core", [(0, 1), (1, 0)])


def on_device(grads, master, moment, second):
    core = lax.axis_index("core")
    place = jnp.stack([core, lax.axis_index("z")]).astype(jnp.int32)
    halves = grads.reshape(X_LO, CORE, Z * Q, WIDTH)
    other = swap(halves)
    own = lax.dynamic_index_in_dim(halves, core, axis=1, keepdims=False)
    pair = pl.pallas_call(
        pair_sum_kernel,
        out_shape=jax.ShapeDtypeStruct((PEERS, Z, WIDTH), BF16),
        in_specs=[scalar(), *vmem(2)],
        out_specs=vmem(1)[0],
        scratch_shapes=[pltpu.VMEM((2, X_LO * Z * Q, 128), F32)],
        compiler_params=SMALL,
    )(place, own, other)
    column = pl.pallas_call(
        plane_sum_kernel,
        out_shape=jax.ShapeDtypeStruct((Z, 16, WIDTH), BF16),
        in_specs=vmem(4),
        out_specs=vmem(1)[0],
        compiler_params=SMALL,
    )(exchange(pair, PLANE), master, moment, second)
    state = jax.ShapeDtypeStruct((1, WIDTH), F32)
    weights, mine = pl.pallas_call(
        update_kernel,
        out_shape=(jax.ShapeDtypeStruct((PEERS, Z, WIDTH), BF16), state),
        in_specs=[scalar(), *vmem(1)],
        out_specs=vmem(2),
        compiler_params=SMALL,
    )(place, exchange(column, "z"))
    gathered = exchange(weights, PLANE)
    all_values = jax.ShapeDtypeStruct((X_LO, CORE, Z * Q, WIDTH), BF16)
    in_order = pltpu.VMEM((2, Z * Q, 128), F32)
    staged = pltpu.VMEM((X_LO, Z * Q, WIDTH), BF16)
    sems = pltpu.SemaphoreType.DMA((X_LO,))
    own_values, own_scales, master_new, moment_new, second_new = pl.pallas_call(
        own_half_kernel,
        out_shape=(all_values, jax.ShapeDtypeStruct((X_LO, Z * Q), F32), state, state, state),
        in_specs=[scalar(), *vmem(5)],
        out_specs=[pl.BlockSpec(memory_space=pltpu.HBM), *vmem(4)],
        scratch_shapes=[in_order, staged, sems],
        compiler_params=SMALL,
        cost_estimate=pl.CostEstimate(flops=400_000, bytes_accessed=2**20, transcendentals=0),
    )(place, gathered, mine, master, moment, second)
    values, scales = pl.pallas_call(
        other_half_kernel,
        out_shape=(all_values, jax.ShapeDtypeStruct((X_LO * CORE, Z * Q), BF16)),
        in_specs=[scalar(), *vmem(2), pl.BlockSpec(memory_space=pltpu.HBM)],
        out_specs=[pl.BlockSpec(memory_space=pltpu.HBM), *vmem(1)],
        scratch_shapes=[in_order, staged, pltpu.VMEM((X_LO * CORE, Z * Q), F32), sems],
        input_output_aliases={3: 0},
        compiler_params=SMALL,
    )(place, own_scales, swap(gathered), own_values)
    return (master_new, moment_new, second_new, values.reshape(-1, WIDTH), scales.reshape(-1))


def solution(mesh):
    devices = Mesh(mesh.devices.reshape(SIZES), AXES)
    rows = P(AXES, None)
    return jax.shard_map(
        on_device,
        mesh=devices,
        in_specs=(P(AXES, None, None), rows, rows, rows),
        out_specs=(rows, rows, rows, P(), P()),
        check_vma=False,
    )
```

```python
import jax
import jax.numpy as jnp
from jax import lax
from jax.experimental import pallas as pl
from jax.experimental.pallas import tpu as pltpu
from jax.sharding import Mesh
from jax.sharding import PartitionSpec as P

EPS_SCALE = 1e-05
BETA_ONE = 0.9
BETA_TWO = 0.95
LEARN_RATE = 0.02
DECAY_RATE = 0.1
EPS_ADAM = 1e-08
CORRECT_ONE = 1.0 - 0.9**10
CORRECT_TWO = 1.0 - 0.95**10

AXES = ("x_lo", "core", "z", "y", "x_hi")
SIZES = (4, 2, 8, 8, 2)
X_LO, CORE, Z, Y, X_HI = SIZES
PLANE = ("y", "x_hi", "x_lo")
Q = Y * X_HI
PEERS = X_LO * Q
WIDTH = 256
F32 = jnp.float32
BF16 = jnp.bfloat16
SMALL = pltpu.CompilerParams(vmem_limit_bytes=8 * 2**20)


def pair_sum_kernel(core_ref, z_ref, own_ref, got_ref, out_ref, total):
    core = core_ref[0]
    for x in range(X_LO):
        rows = pl.ds(x * Z * Q, Z * Q)
        both = own_ref[x].astype(F32) + got_ref[x, core].astype(F32)
        for half in range(2):
            total[half, rows, :] = both[:, half * 128 : half * 128 + 128]
    for x in range(X_LO):
        for q in range(Q):
            for half in range(2):
                picked = total[half, pl.ds(x * Z * Q + q, Z, stride=Q), :]
                out_ref[q * X_LO + x, :, half * 128 : half * 128 + 128] = picked.astype(BF16)


def pieces(values, count):
    parts = []
    for _ in range(count):
        parts.append(values.astype(BF16).astype(F32))
        values = values - parts[-1]
    return parts


def plane_sum_kernel(got_ref, master_ref, moment_ref, second_ref, out_ref):
    lanes = [got_ref[p].astype(F32) for p in range(8)]
    for p in range(8, PEERS):
        lanes[p % 8] = lanes[p % 8] + got_ref[p].astype(F32)
    while len(lanes) > 1:
        lanes = [a + b for a, b in zip(lanes[::2], lanes[1::2])]
    parts = [*pieces(master_ref[...], 3), *pieces(moment_ref[...], 2), *pieces(second_ref[...], 2)]
    parts.append(jnp.zeros((1, WIDTH), F32))
    rows = jnp.concatenate([lanes[0], *parts], axis=0).astype(BF16)
    for p in range(Z):
        out_ref[p] = rows


def adamw(master, moment, second, summed):
    moment_new = BETA_ONE * moment + (1.0 - BETA_ONE) * summed
    second_new = BETA_TWO * second + (1.0 - BETA_TWO) * summed * summed
    update = moment_new / CORRECT_ONE / (jnp.sqrt(second_new / CORRECT_TWO) + EPS_ADAM)
    return master - LEARN_RATE * (update + DECAY_RATE * master), moment_new, second_new


def update_kernel(z_ref, got_ref, out_ref, mine_ref):
    got = [got_ref[p].astype(F32) for p in range(Z)]
    summed = got[0][0:8]
    for p in range(1, Z):
        summed = summed + got[p][0:8]
    row = lax.broadcasted_iota(jnp.int32, (Z, WIDTH), 0)

    def state(first, count):
        rows = jnp.zeros((Z, WIDTH), F32)
        for p in range(Z):
            value = got[p][first : first + 1]
            for k in range(1, count):
                value = value + got[p][first + k : first + k + 1]
            rows = jnp.where(row == p, value, rows)
        return rows

    sent = adamw(state(8, 3), state(11, 2), state(13, 2), summed)[0].astype(BF16)
    for p in range(PEERS):
        out_ref[p] = sent
    mine_ref[...] = jnp.sum(jnp.where(row == z_ref[0], summed, 0.0), axis=0, keepdims=True)


def quantize_half(ref, write, rows_in_order):
    lane = lax.broadcasted_iota(jnp.int32, (Z, 128), 1)
    row = lax.broadcasted_iota(jnp.int32, (Z, 128), 0)
    for x in range(X_LO):
        spread = jnp.zeros((Z, 128), F32)
        for q in range(Q):
            weights = ref[q * X_LO + x].astype(F32)
            scale = (jnp.max(jnp.abs(weights), axis=-1, keepdims=True) + EPS_SCALE).astype(BF16).astype(F32)
            values = weights / scale
            for half in range(2):
                rows_in_order[half, pl.ds(q, Z, stride=Q), :] = values[:, half * 128 : half * 128 + 128]
            spread = jnp.where(lane % Q == q, scale, spread)
        write(x, jnp.sum(jnp.where(lane // Q == row, spread, 0.0), axis=0, keepdims=True))


def own_half_kernel(
    own_ref, mine_ref, master_in, moment_in, second_in,
    values_ref, scales_ref, master_ref, moment_ref, second_ref, rows_in_order,
):
    def write(x, scales):
        for half in range(2):
            values_ref[x, :, half * 128 : half * 128 + 128] = rows_in_order[half].astype(BF16)
        scales_ref[x : x + 1, :] = scales

    own = adamw(master_in[...], moment_in[...], second_in[...], mine_ref[...])
    master_ref[...], moment_ref[...], second_ref[...] = own
    quantize_half(own_ref, write, rows_in_order)


def other_half_kernel(core_ref, own_values_ref, own_scales_ref, got_ref, values_ref, scales_ref, rows_in_order, scale_rows):
    core = core_ref[0]
    for x in range(X_LO):
        values_ref[x, core] = own_values_ref[x]
        scale_rows[pl.ds(x * CORE + core, 1), :] = own_scales_ref[x : x + 1, :]

    def write(x, scales):
        for half in range(2):
            values_ref[x, 1 - core, :, half * 128 : half * 128 + 128] = rows_in_order[half].astype(BF16)
        scale_rows[pl.ds(x * CORE + 1 - core, 1), :] = scales

    quantize_half(got_ref, write, rows_in_order)
    scales_ref[...] = scale_rows[...].astype(BF16)


def vmem(count):
    return [pl.BlockSpec(memory_space=pltpu.VMEM)] * count


def scalar():
    return pl.BlockSpec(memory_space=pltpu.SMEM)


def exchange(rows, axis):
    return lax.all_to_all(rows, axis, split_axis=0, concat_axis=0, tiled=True)


def swap(rows):
    return lax.ppermute(rows, "core", [(0, 1), (1, 0)])


def on_device(grads, master, moment, second):
    core = lax.axis_index("core")
    core_index = core.astype(jnp.int32)[None]
    z_index = lax.axis_index("z").astype(jnp.int32)[None]
    halves = grads.reshape(X_LO, CORE, Z * Q, WIDTH)
    other = swap(halves)
    own = lax.dynamic_index_in_dim(halves, core, axis=1, keepdims=False)
    pair = pl.pallas_call(
        pair_sum_kernel,
        out_shape=jax.ShapeDtypeStruct((PEERS, Z, WIDTH), BF16),
        in_specs=[scalar(), scalar(), *vmem(2)],
        out_specs=vmem(1)[0],
        scratch_shapes=[pltpu.VMEM((2, X_LO * Z * Q, 128), F32)],
        compiler_params=SMALL,
    )(core_index, z_index, own, other)
    column = pl.pallas_call(
        plane_sum_kernel,
        out_shape=jax.ShapeDtypeStruct((Z, 16, WIDTH), BF16),
        in_specs=vmem(4),
        out_specs=vmem(1)[0],
        compiler_params=SMALL,
    )(exchange(pair, PLANE), master, moment, second)
    state = jax.ShapeDtypeStruct((1, WIDTH), F32)
    weights, mine = pl.pallas_call(
        update_kernel,
        out_shape=(jax.ShapeDtypeStruct((PEERS, Z, WIDTH), BF16), state),
        in_specs=[scalar(), *vmem(1)],
        out_specs=vmem(2),
        compiler_params=SMALL,
    )(z_index, exchange(column, "z"))
    gathered = exchange(weights, PLANE)
    in_order = pltpu.VMEM((2, Z * Q, 128), F32)
    own_values, own_scales, master_new, moment_new, second_new = pl.pallas_call(
        own_half_kernel,
        out_shape=(
            jax.ShapeDtypeStruct((X_LO, Z * Q, WIDTH), BF16),
            jax.ShapeDtypeStruct((X_LO, Z * Q), F32),
            state,
            state,
            state,
        ),
        in_specs=vmem(5),
        out_specs=vmem(5),
        scratch_shapes=[in_order],
        compiler_params=SMALL,
        cost_estimate=pl.CostEstimate(flops=400_000, bytes_accessed=2**20, transcendentals=0),
    )(gathered, mine, master, moment, second)
    values, scales = pl.pallas_call(
        other_half_kernel,
        out_shape=(
            jax.ShapeDtypeStruct((X_LO, CORE, Z * Q, WIDTH), BF16),
            jax.ShapeDtypeStruct((X_LO * CORE, Z * Q), BF16),
        ),
        in_specs=[scalar(), *vmem(3)],
        out_specs=vmem(2),
        scratch_shapes=[in_order, pltpu.VMEM((X_LO * CORE, Z * Q), F32)],
        compiler_params=SMALL,
    )(core_index, own_values, own_scales, swap(gathered))
    return (master_new, moment_new, second_new, values.reshape(-1, WIDTH), scales.reshape(-1))


def solution(mesh):
    devices = Mesh(mesh.devices.reshape(SIZES), AXES)
    rows = P(AXES, None)
    return jax.shard_map(
        on_device,
        mesh=devices,
        in_specs=(P(AXES, None, None), rows, rows, rows),
        out_specs=(rows, rows, rows, P(), P()),
        check_vma=False,
    )
```

```python
import jax
import jax.numpy as jnp
from jax import lax
from jax.experimental import pallas as pl
from jax.experimental.pallas import tpu as pltpu
from jax.sharding import Mesh
from jax.sharding import PartitionSpec as P

EPS_SCALE = 1e-05
BETA_ONE = 0.9
BETA_TWO = 0.95
LEARN_RATE = 0.02
DECAY_RATE = 0.1
EPS_ADAM = 1e-08
CORRECT_ONE = 1.0 - 0.9**10
CORRECT_TWO = 1.0 - 0.95**10

AXES = ("x_lo", "core", "z", "y", "x_hi")
SIZES = (4, 2, 8, 8, 2)
X_LO, CORE, Z, Y, X_HI = SIZES
PLANE = ("y", "x_hi", "x_lo")
Q = Y * X_HI
PEERS = X_LO * Q
WIDTH = 256
F32 = jnp.float32
BF16 = jnp.bfloat16
SMALL = pltpu.CompilerParams(vmem_limit_bytes=8 * 2**20)


def pair_sum_kernel(core_ref, z_ref, both_ref, out_ref, total):
    core = core_ref[0]
    for x in range(X_LO):
        rows = pl.ds(x * Z * Q, Z * Q)
        both = both_ref[0, x, core].astype(F32) + both_ref[1, x, core].astype(F32)
        for half in range(2):
            total[half, rows, :] = both[:, half * 128 : half * 128 + 128]
    for x in range(X_LO):
        for q in range(Q):
            for half in range(2):
                picked = total[half, pl.ds(x * Z * Q + q, Z, stride=Q), :]
                out_ref[q * X_LO + x, :, half * 128 : half * 128 + 128] = picked.astype(BF16)


def pieces(values, count):
    parts = []
    for _ in range(count):
        parts.append(values.astype(BF16).astype(F32))
        values = values - parts[-1]
    return parts


def plane_sum_kernel(got_ref, master_ref, moment_ref, second_ref, out_ref):
    lanes = [got_ref[p].astype(F32) for p in range(8)]
    for p in range(8, PEERS):
        lanes[p % 8] = lanes[p % 8] + got_ref[p].astype(F32)
    while len(lanes) > 1:
        lanes = [a + b for a, b in zip(lanes[::2], lanes[1::2])]
    parts = [*pieces(master_ref[...], 3), *pieces(moment_ref[...], 2), *pieces(second_ref[...], 2)]
    parts.append(jnp.zeros((1, WIDTH), F32))
    rows = jnp.concatenate([lanes[0], *parts], axis=0).astype(BF16)
    for p in range(Z):
        out_ref[p] = rows


def adamw(master, moment, second, summed):
    moment_new = BETA_ONE * moment + (1.0 - BETA_ONE) * summed
    second_new = BETA_TWO * second + (1.0 - BETA_TWO) * summed * summed
    update = moment_new / CORRECT_ONE / (jnp.sqrt(second_new / CORRECT_TWO) + EPS_ADAM)
    return master - LEARN_RATE * (update + DECAY_RATE * master), moment_new, second_new


def update_kernel(z_ref, got_ref, out_ref, mine_ref):
    got = [got_ref[p].astype(F32) for p in range(Z)]
    summed = got[0][0:8]
    for p in range(1, Z):
        summed = summed + got[p][0:8]
    row = lax.broadcasted_iota(jnp.int32, (Z, WIDTH), 0)

    def state(first, count):
        rows = jnp.zeros((Z, WIDTH), F32)
        for p in range(Z):
            value = got[p][first : first + 1]
            for k in range(1, count):
                value = value + got[p][first + k : first + k + 1]
            rows = jnp.where(row == p, value, rows)
        return rows

    sent = adamw(state(8, 3), state(11, 2), state(13, 2), summed)[0].astype(BF16)
    for p in range(PEERS):
        out_ref[p] = sent
    mine_ref[...] = jnp.sum(jnp.where(row == z_ref[0], summed, 0.0), axis=0, keepdims=True)


def quantize_kernel(
    both_ref, mine_ref, master_in, moment_in, second_in,
    values_ref, scales_ref, master_ref, moment_ref, second_ref, rows_in_order, scale_rows,
):
    own = adamw(master_in[...], moment_in[...], second_in[...], mine_ref[...])
    master_ref[...], moment_ref[...], second_ref[...] = own
    lane = lax.broadcasted_iota(jnp.int32, (Z, 128), 1)
    row = lax.broadcasted_iota(jnp.int32, (Z, 128), 0)
    for x in range(X_LO):
        for core in range(CORE):
            spread = jnp.zeros((Z, 128), F32)
            for q in range(Q):
                weights = both_ref[core, q * X_LO + x].astype(F32)
                scale = (jnp.max(jnp.abs(weights), axis=-1, keepdims=True) + EPS_SCALE).astype(BF16).astype(F32)
                values = weights / scale
                for half in range(2):
                    rows_in_order[half, pl.ds(q, Z, stride=Q), :] = values[:, half * 128 : half * 128 + 128]
                spread = jnp.where(lane % Q == q, scale, spread)
            for half in range(2):
                values_ref[x, core, :, half * 128 : half * 128 + 128] = rows_in_order[half].astype(BF16)
            at = x * CORE + core
            scale_rows[at : at + 1, :] = jnp.sum(jnp.where(lane // Q == row, spread, 0.0), axis=0, keepdims=True)
    scales_ref[...] = scale_rows[...].astype(BF16)


def vmem(count):
    return [pl.BlockSpec(memory_space=pltpu.VMEM)] * count


def scalar():
    return pl.BlockSpec(memory_space=pltpu.SMEM)


def exchange(rows, axis):
    return lax.all_to_all(rows, axis, split_axis=0, concat_axis=0, tiled=True)


def both_cores(rows):
    return lax.all_gather(rows, "core", axis=0, tiled=False)


def on_device(grads, master, moment, second):
    core_index = lax.axis_index("core").astype(jnp.int32)[None]
    z_index = lax.axis_index("z").astype(jnp.int32)[None]
    halves = grads.reshape(X_LO, CORE, Z * Q, WIDTH)
    pair = pl.pallas_call(
        pair_sum_kernel,
        out_shape=jax.ShapeDtypeStruct((PEERS, Z, WIDTH), BF16),
        in_specs=[scalar(), scalar(), *vmem(1)],
        out_specs=vmem(1)[0],
        scratch_shapes=[pltpu.VMEM((2, X_LO * Z * Q, 128), F32)],
        compiler_params=SMALL,
    )(core_index, z_index, both_cores(halves))
    column = pl.pallas_call(
        plane_sum_kernel,
        out_shape=jax.ShapeDtypeStruct((Z, 16, WIDTH), BF16),
        in_specs=vmem(4),
        out_specs=vmem(1)[0],
        compiler_params=SMALL,
    )(exchange(pair, PLANE), master, moment, second)
    state = jax.ShapeDtypeStruct((1, WIDTH), F32)
    weights, mine = pl.pallas_call(
        update_kernel,
        out_shape=(jax.ShapeDtypeStruct((PEERS, Z, WIDTH), BF16), state),
        in_specs=[scalar(), *vmem(1)],
        out_specs=vmem(2),
        compiler_params=SMALL,
    )(z_index, exchange(column, "z"))
    gathered = both_cores(exchange(weights, PLANE))
    values, scales, master_new, moment_new, second_new = pl.pallas_call(
        quantize_kernel,
        out_shape=(
            jax.ShapeDtypeStruct((X_LO, CORE, Z * Q, WIDTH), BF16),
            jax.ShapeDtypeStruct((X_LO * CORE, Z * Q), BF16),
            state,
            state,
            state,
        ),
        in_specs=vmem(5),
        out_specs=vmem(5),
        scratch_shapes=[pltpu.VMEM((2, Z * Q, 128), F32), pltpu.VMEM((X_LO * CORE, Z * Q), F32)],
        compiler_params=SMALL,
    )(gathered, mine, master, moment, second)
    return (master_new, moment_new, second_new, values.reshape(-1, WIDTH), scales.reshape(-1))


def solution(mesh):
    devices = Mesh(mesh.devices.reshape(SIZES), AXES)
    rows = P(AXES, None)
    return jax.shard_map(
        on_device,
        mesh=devices,
        in_specs=(P(AXES, None, None), rows, rows, rows),
        out_specs=(rows, rows, rows, P(), P()),
        check_vma=False,
    )
```

```python
import jax
import jax.numpy as jnp
from jax import lax
from jax.experimental import pallas as pl
from jax.experimental.pallas import tpu as pltpu
from jax.sharding import Mesh
from jax.sharding import PartitionSpec as P

EPS_SCALE = 1e-05
BETA_ONE = 0.9
BETA_TWO = 0.95
LEARN_RATE = 0.02
DECAY_RATE = 0.1
EPS_ADAM = 1e-08
CORRECT_ONE = 1.0 - 0.9**10
CORRECT_TWO = 1.0 - 0.95**10

AXES = ("x_lo", "core", "z", "y", "x_hi")
SIZES = (4, 2, 8, 8, 2)
X_LO, CORE, Z, Y, X_HI = SIZES
PLANE = ("y", "x_hi", "x_lo")
Q = Y * X_HI
PEERS = X_LO * Q
WIDTH = 256
F32 = jnp.float32
BF16 = jnp.bfloat16
SMALL = pltpu.CompilerParams(vmem_limit_bytes=8 * 2**20)


def lay_out_kernel(z_ref, grads_ref, out_ref, wide):
    for x in range(X_LO):
        for core in range(CORE):
            for half in range(2):
                wide[half] = grads_ref[x, core, :, half * 128 : half * 128 + 128].astype(F32)
            for q in range(Q):
                for half in range(2):
                    picked = wide[half, pl.ds(q, Z, stride=Q), :]
                    out_ref[core, q * X_LO + x, :, half * 128 : half * 128 + 128] = picked.astype(BF16)


def pair_sum_kernel(both_ref, out_ref):
    for p in range(PEERS):
        out_ref[p] = (both_ref[0, p].astype(F32) + both_ref[1, p].astype(F32)).astype(BF16)


def pieces(values, count):
    parts = []
    for _ in range(count):
        parts.append(values.astype(BF16).astype(F32))
        values = values - parts[-1]
    return parts


def plane_sum_kernel(got_ref, master_ref, moment_ref, second_ref, out_ref):
    lanes = [got_ref[p].astype(F32) for p in range(8)]
    for p in range(8, PEERS):
        lanes[p % 8] = lanes[p % 8] + got_ref[p].astype(F32)
    while len(lanes) > 1:
        lanes = [a + b for a, b in zip(lanes[::2], lanes[1::2])]
    parts = [*pieces(master_ref[...], 3), *pieces(moment_ref[...], 2), *pieces(second_ref[...], 2)]
    parts.append(jnp.zeros((1, WIDTH), F32))
    rows = jnp.concatenate([lanes[0], *parts], axis=0).astype(BF16)
    for p in range(Z):
        out_ref[p] = rows


def adamw(master, moment, second, summed):
    moment_new = BETA_ONE * moment + (1.0 - BETA_ONE) * summed
    second_new = BETA_TWO * second + (1.0 - BETA_TWO) * summed * summed
    update = moment_new / CORRECT_ONE / (jnp.sqrt(second_new / CORRECT_TWO) + EPS_ADAM)
    return master - LEARN_RATE * (update + DECAY_RATE * master), moment_new, second_new


def update_kernel(z_ref, got_ref, out_ref, mine_ref):
    got = [got_ref[p].astype(F32) for p in range(Z)]
    summed = got[0][0:8]
    for p in range(1, Z):
        summed = summed + got[p][0:8]
    row = lax.broadcasted_iota(jnp.int32, (Z, WIDTH), 0)

    def state(first, count):
        rows = jnp.zeros((Z, WIDTH), F32)
        for p in range(Z):
            value = got[p][first : first + 1]
            for k in range(1, count):
                value = value + got[p][first + k : first + k + 1]
            rows = jnp.where(row == p, value, rows)
        return rows

    sent = adamw(state(8, 3), state(11, 2), state(13, 2), summed)[0].astype(BF16)
    for p in range(PEERS):
        out_ref[p] = sent
    mine_ref[...] = jnp.sum(jnp.where(row == z_ref[0], summed, 0.0), axis=0, keepdims=True)


def quantize_kernel(
    both_ref, mine_ref, master_in, moment_in, second_in,
    values_ref, scales_ref, master_ref, moment_ref, second_ref, rows_in_order, scale_rows,
):
    own = adamw(master_in[...], moment_in[...], second_in[...], mine_ref[...])
    master_ref[...], moment_ref[...], second_ref[...] = own
    lane = lax.broadcasted_iota(jnp.int32, (Z, 128), 1)
    row = lax.broadcasted_iota(jnp.int32, (Z, 128), 0)
    for x in range(X_LO):
        for core in range(CORE):
            spread = jnp.zeros((Z, 128), F32)
            for q in range(Q):
                weights = both_ref[core, q * X_LO + x].astype(F32)
                scale = (jnp.max(jnp.abs(weights), axis=-1, keepdims=True) + EPS_SCALE).astype(BF16).astype(F32)
                values = weights / scale
                for half in range(2):
                    rows_in_order[half, pl.ds(q, Z, stride=Q), :] = values[:, half * 128 : half * 128 + 128]
                spread = jnp.where(lane % Q == q, scale, spread)
            for half in range(2):
                values_ref[x, core, :, half * 128 : half * 128 + 128] = rows_in_order[half].astype(BF16)
            at = x * CORE + core
            scale_rows[at : at + 1, :] = jnp.sum(jnp.where(lane // Q == row, spread, 0.0), axis=0, keepdims=True)
    scales_ref[...] = scale_rows[...].astype(BF16)


def vmem(count):
    return [pl.BlockSpec(memory_space=pltpu.VMEM)] * count


def scalar():
    return pl.BlockSpec(memory_space=pltpu.SMEM)


def exchange(rows, axis):
    return lax.all_to_all(rows, axis, split_axis=0, concat_axis=0, tiled=True)


def both_cores(rows):
    return lax.all_gather(rows, "core", axis=0, tiled=False)


def on_device(grads, master, moment, second):
    z_index = lax.axis_index("z").astype(jnp.int32)[None]
    laid_out = pl.pallas_call(
        lay_out_kernel,
        out_shape=jax.ShapeDtypeStruct((CORE, PEERS, Z, WIDTH), BF16),
        in_specs=[scalar(), *vmem(1)],
        out_specs=vmem(1)[0],
        scratch_shapes=[pltpu.VMEM((2, Z * Q, 128), F32)],
        compiler_params=SMALL,
    )(z_index, grads.reshape(X_LO, CORE, Z * Q, WIDTH))
    pair = pl.pallas_call(
        pair_sum_kernel,
        out_shape=jax.ShapeDtypeStruct((PEERS, Z, WIDTH), BF16),
        in_specs=vmem(1),
        out_specs=vmem(1)[0],
        compiler_params=SMALL,
    )(exchange(laid_out, "core"))
    column = pl.pallas_call(
        plane_sum_kernel,
        out_shape=jax.ShapeDtypeStruct((Z, 16, WIDTH), BF16),
        in_specs=vmem(4),
        out_specs=vmem(1)[0],
        compiler_params=SMALL,
    )(exchange(pair, PLANE), master, moment, second)
    state = jax.ShapeDtypeStruct((1, WIDTH), F32)
    weights, mine = pl.pallas_call(
        update_kernel,
        out_shape=(jax.ShapeDtypeStruct((PEERS, Z, WIDTH), BF16), state),
        in_specs=[scalar(), *vmem(1)],
        out_specs=vmem(2),
        compiler_params=SMALL,
    )(z_index, exchange(column, "z"))
    gathered = both_cores(exchange(weights, PLANE))
    values, scales, master_new, moment_new, second_new = pl.pallas_call(
        quantize_kernel,
        out_shape=(
            jax.ShapeDtypeStruct((X_LO, CORE, Z * Q, WIDTH), BF16),
            jax.ShapeDtypeStruct((X_LO * CORE, Z * Q), BF16),
            state,
            state,
            state,
        ),
        in_specs=vmem(5),
        out_specs=vmem(5),
        scratch_shapes=[pltpu.VMEM((2, Z * Q, 128), F32), pltpu.VMEM((X_LO * CORE, Z * Q), F32)],
        compiler_params=SMALL,
    )(gathered, mine, master, moment, second)
    return (master_new, moment_new, second_new, values.reshape(-1, WIDTH), scales.reshape(-1))


def solution(mesh):
    devices = Mesh(mesh.devices.reshape(SIZES), AXES)
    rows = P(AXES, None)
    return jax.shard_map(
        on_device,
        mesh=devices,
        in_specs=(P(AXES, None, None), rows, rows, rows),
        out_specs=(rows, rows, rows, P(), P()),
        check_vma=False,
    )
```

```python
import jax
import jax.numpy as jnp
from jax import lax
from jax.experimental import pallas as pl
from jax.experimental.pallas import tpu as pltpu
from jax.sharding import Mesh
from jax.sharding import PartitionSpec as P

EPS_SCALE = 1e-05
BETA_ONE = 0.9
BETA_TWO = 0.95
LEARN_RATE = 0.02
DECAY_RATE = 0.1
EPS_ADAM = 1e-08
CORRECT_ONE = 1.0 - 0.9**10
CORRECT_TWO = 1.0 - 0.95**10

AXES = ("x_lo", "core", "z", "y", "x_hi")
SIZES = (4, 2, 8, 8, 2)
X_LO, CORE, Z, Y, X_HI = SIZES
PLANE = ("y", "x_hi", "x_lo")
Q = Y * X_HI
PEERS = X_LO * Q
WIDTH = 256
F32 = jnp.float32
BF16 = jnp.bfloat16
SMALL = pltpu.CompilerParams(vmem_limit_bytes=8 * 2**20)


def split_kernel(core_ref, z_ref, grads_ref, send_ref, own_ref, sems):
    core = core_ref[0]
    copies = [
        pltpu.make_async_copy(grads_ref.at[:, 1 - core], send_ref, sems.at[0]),
        pltpu.make_async_copy(grads_ref.at[:, core], own_ref, sems.at[1]),
    ]
    for copy in copies:
        copy.start()
    for copy in copies:
        copy.wait()


def pair_sum_kernel(core_ref, own_ref, sent_ref, out_ref, total):
    core = core_ref[0]
    for x in range(X_LO):
        rows = pl.ds(x * Z * Q, Z * Q)
        both = own_ref[x].astype(F32) + sent_ref[1 - core, x].astype(F32)
        for half in range(2):
            total[half, rows, :] = both[:, half * 128 : half * 128 + 128]
    for x in range(X_LO):
        for q in range(Q):
            for half in range(2):
                picked = total[half, pl.ds(x * Z * Q + q, Z, stride=Q), :]
                out_ref[q * X_LO + x, :, half * 128 : half * 128 + 128] = picked.astype(BF16)


def pieces(values, count):
    parts = []
    for _ in range(count):
        parts.append(values.astype(BF16).astype(F32))
        values = values - parts[-1]
    return parts


def plane_sum_kernel(got_ref, master_ref, moment_ref, second_ref, out_ref):
    lanes = [got_ref[p].astype(F32) for p in range(8)]
    for p in range(8, PEERS):
        lanes[p % 8] = lanes[p % 8] + got_ref[p].astype(F32)
    while len(lanes) > 1:
        lanes = [a + b for a, b in zip(lanes[::2], lanes[1::2])]
    parts = [*pieces(master_ref[...], 3), *pieces(moment_ref[...], 2), *pieces(second_ref[...], 2)]
    parts.append(jnp.zeros((1, WIDTH), F32))
    rows = jnp.concatenate([lanes[0], *parts], axis=0).astype(BF16)
    for p in range(Z):
        out_ref[p] = rows


def adamw(master, moment, second, summed):
    moment_new = BETA_ONE * moment + (1.0 - BETA_ONE) * summed
    second_new = BETA_TWO * second + (1.0 - BETA_TWO) * summed * summed
    update = moment_new / CORRECT_ONE / (jnp.sqrt(second_new / CORRECT_TWO) + EPS_ADAM)
    return master - LEARN_RATE * (update + DECAY_RATE * master), moment_new, second_new


def update_kernel(z_ref, got_ref, out_ref, mine_ref):
    got = [got_ref[p].astype(F32) for p in range(Z)]
    summed = got[0][0:8]
    for p in range(1, Z):
        summed = summed + got[p][0:8]
    row = lax.broadcasted_iota(jnp.int32, (Z, WIDTH), 0)

    def state(first, count):
        rows = jnp.zeros((Z, WIDTH), F32)
        for p in range(Z):
            value = got[p][first : first + 1]
            for k in range(1, count):
                value = value + got[p][first + k : first + k + 1]
            rows = jnp.where(row == p, value, rows)
        return rows

    sent = adamw(state(8, 3), state(11, 2), state(13, 2), summed)[0].astype(BF16)
    for p in range(PEERS):
        out_ref[p] = sent
    mine_ref[...] = jnp.sum(jnp.where(row == z_ref[0], summed, 0.0), axis=0, keepdims=True)


def quantize_kernel(
    both_ref, mine_ref, master_in, moment_in, second_in,
    values_ref, scales_ref, master_ref, moment_ref, second_ref, rows_in_order, scale_rows,
):
    own = adamw(master_in[...], moment_in[...], second_in[...], mine_ref[...])
    master_ref[...], moment_ref[...], second_ref[...] = own
    lane = lax.broadcasted_iota(jnp.int32, (Z, 128), 1)
    row = lax.broadcasted_iota(jnp.int32, (Z, 128), 0)
    for x in range(X_LO):
        for core in range(CORE):
            spread = jnp.zeros((Z, 128), F32)
            for q in range(Q):
                weights = both_ref[core, q * X_LO + x].astype(F32)
                scale = (jnp.max(jnp.abs(weights), axis=-1, keepdims=True) + EPS_SCALE).astype(BF16).astype(F32)
                values = weights / scale
                for half in range(2):
                    rows_in_order[half, pl.ds(q, Z, stride=Q), :] = values[:, half * 128 : half * 128 + 128]
                spread = jnp.where(lane % Q == q, scale, spread)
            for half in range(2):
                values_ref[x, core, :, half * 128 : half * 128 + 128] = rows_in_order[half].astype(BF16)
            at = x * CORE + core
            scale_rows[at : at + 1, :] = jnp.sum(jnp.where(lane // Q == row, spread, 0.0), axis=0, keepdims=True)
    scales_ref[...] = scale_rows[...].astype(BF16)


def vmem(count):
    return [pl.BlockSpec(memory_space=pltpu.VMEM)] * count


def scalar():
    return pl.BlockSpec(memory_space=pltpu.SMEM)


def exchange(rows, axis):
    return lax.all_to_all(rows, axis, split_axis=0, concat_axis=0, tiled=True)


def both_cores(rows):
    return lax.all_gather(rows, "core", axis=0, tiled=False)


def on_device(grads, master, moment, second):
    core_index = lax.axis_index("core").astype(jnp.int32)[None]
    z_index = lax.axis_index("z").astype(jnp.int32)[None]
    half = jax.ShapeDtypeStruct((X_LO, Z * Q, WIDTH), BF16)
    send, own = pl.pallas_call(
        split_kernel,
        out_shape=(half, half),
        in_specs=[scalar(), scalar(), pl.BlockSpec(memory_space=pltpu.HBM)],
        out_specs=vmem(2),
        scratch_shapes=[pltpu.SemaphoreType.DMA((2,))],
        compiler_params=SMALL,
    )(core_index, z_index, grads.reshape(X_LO, CORE, Z * Q, WIDTH))
    pair = pl.pallas_call(
        pair_sum_kernel,
        out_shape=jax.ShapeDtypeStruct((PEERS, Z, WIDTH), BF16),
        in_specs=[scalar(), *vmem(2)],
        out_specs=vmem(1)[0],
        scratch_shapes=[pltpu.VMEM((2, X_LO * Z * Q, 128), F32)],
        compiler_params=SMALL,
    )(core_index, own, both_cores(send))
    column = pl.pallas_call(
        plane_sum_kernel,
        out_shape=jax.ShapeDtypeStruct((Z, 16, WIDTH), BF16),
        in_specs=vmem(4),
        out_specs=vmem(1)[0],
        compiler_params=SMALL,
    )(exchange(pair, PLANE), master, moment, second)
    state = jax.ShapeDtypeStruct((1, WIDTH), F32)
    weights, mine = pl.pallas_call(
        update_kernel,
        out_shape=(jax.ShapeDtypeStruct((PEERS, Z, WIDTH), BF16), state),
        in_specs=[scalar(), *vmem(1)],
        out_specs=vmem(2),
        compiler_params=SMALL,
    )(z_index, exchange(column, "z"))
    gathered = both_cores(exchange(weights, PLANE))
    values, scales, master_new, moment_new, second_new = pl.pallas_call(
        quantize_kernel,
        out_shape=(
            jax.ShapeDtypeStruct((X_LO, CORE, Z * Q, WIDTH), BF16),
            jax.ShapeDtypeStruct((X_LO * CORE, Z * Q), BF16),
            state,
            state,
            state,
        ),
        in_specs=vmem(5),
        out_specs=vmem(5),
        scratch_shapes=[pltpu.VMEM((2, Z * Q, 128), F32), pltpu.VMEM((X_LO * CORE, Z * Q), F32)],
        compiler_params=SMALL,
    )(gathered, mine, master, moment, second)
    return (master_new, moment_new, second_new, values.reshape(-1, WIDTH), scales.reshape(-1))


def solution(mesh):
    devices = Mesh(mesh.devices.reshape(SIZES), AXES)
    rows = P(AXES, None)
    return jax.shard_map(
        on_device,
        mesh=devices,
        in_specs=(P(AXES, None, None), rows, rows, rows),
        out_specs=(rows, rows, rows, P(), P()),
        check_vma=False,
    )
```

```python
import jax
import jax.numpy as jnp
from jax import lax
from jax.experimental import pallas as pl
from jax.experimental.pallas import tpu as pltpu
from jax.sharding import Mesh
from jax.sharding import PartitionSpec as P

EPS_SCALE = 1e-05
BETA_ONE = 0.9
BETA_TWO = 0.95
LEARN_RATE = 0.02
DECAY_RATE = 0.1
EPS_ADAM = 1e-08
CORRECT_ONE = 1.0 - 0.9**10
CORRECT_TWO = 1.0 - 0.95**10

X_LO, CORE, Z, Y, X_HI = 4, 2, 8, 8, 2
Q = Y * X_HI
PEERS = X_LO * Q
WIDTH = 256
F32 = jnp.float32
BF16 = jnp.bfloat16
SMALL = pltpu.CompilerParams(vmem_limit_bytes=8 * 2**20)


def split_kernel(pipe_ref, z_ref, grads_ref, send_ref, own_ref):
    row = lax.broadcasted_iota(jnp.int32, (Z * Q, WIDTH), 0)
    swapped = ((row % X_HI) + row // (Z * Q // 2) + pipe_ref[0]) % 2 == 1
    for x in range(X_LO):
        first, second = grads_ref[x, 0].astype(F32), grads_ref[x, 1].astype(F32)
        own_ref[x] = jnp.where(swapped, second, first).astype(BF16)
        send_ref[x] = jnp.where(swapped, first, second).astype(BF16)


def pair_sum_kernel(pipe_ref, own_ref, sent_ref, out_ref, total):
    other = 1 - pipe_ref[0]
    for x in range(X_LO):
        rows = pl.ds(x * Z * Q, Z * Q)
        both = own_ref[x].astype(F32) + sent_ref[other, x].astype(F32)
        for half in range(2):
            total[half, rows, :] = both[:, half * 128 : half * 128 + 128]
    for x in range(X_LO):
        for q in range(Q):
            for half in range(2):
                picked = total[half, pl.ds(x * Z * Q + q, Z, stride=Q), :]
                out_ref[q * X_LO + x, :, half * 128 : half * 128 + 128] = picked.astype(BF16)


def pieces(values, count):
    parts = []
    for _ in range(count):
        parts.append(values.astype(BF16).astype(F32))
        values = values - parts[-1]
    return parts


def plane_sum_kernel(got_ref, master_ref, moment_ref, second_ref, out_ref):
    lanes = [got_ref[p].astype(F32) for p in range(8)]
    for p in range(8, PEERS):
        lanes[p % 8] = lanes[p % 8] + got_ref[p].astype(F32)
    while len(lanes) > 1:
        lanes = [a + b for a, b in zip(lanes[::2], lanes[1::2])]
    parts = [*pieces(master_ref[...], 3), *pieces(moment_ref[...], 2), *pieces(second_ref[...], 2)]
    parts.append(jnp.zeros((1, WIDTH), F32))
    rows = jnp.concatenate([lanes[0], *parts], axis=0).astype(BF16)
    for p in range(Z):
        out_ref[p] = rows


def adamw(master, moment, second, summed):
    moment_new = BETA_ONE * moment + (1.0 - BETA_ONE) * summed
    second_new = BETA_TWO * second + (1.0 - BETA_TWO) * summed * summed
    update = moment_new / CORRECT_ONE / (jnp.sqrt(second_new / CORRECT_TWO) + EPS_ADAM)
    return master - LEARN_RATE * (update + DECAY_RATE * master), moment_new, second_new


def update_kernel(z_ref, got_ref, out_ref, mine_ref):
    got = [got_ref[p].astype(F32) for p in range(Z)]
    summed = got[0][0:8]
    for p in range(1, Z):
        summed = summed + got[p][0:8]
    row = lax.broadcasted_iota(jnp.int32, (Z, WIDTH), 0)

    def state(first, count):
        rows = jnp.zeros((Z, WIDTH), F32)
        for p in range(Z):
            value = got[p][first : first + 1]
            for k in range(1, count):
                value = value + got[p][first + k : first + k + 1]
            rows = jnp.where(row == p, value, rows)
        return rows

    sent = adamw(state(8, 3), state(11, 2), state(13, 2), summed)[0].astype(BF16)
    for p in range(PEERS):
        out_ref[p] = sent
    mine_ref[...] = jnp.sum(jnp.where(row == z_ref[0], summed, 0.0), axis=0, keepdims=True)


def quantize_kernel(
    both_ref, mine_ref, master_in, moment_in, second_in,
    values_ref, scales_ref, master_ref, moment_ref, second_ref, rows_in_order, scale_rows,
):
    own = adamw(master_in[...], moment_in[...], second_in[...], mine_ref[...])
    master_ref[...], moment_ref[...], second_ref[...] = own
    lane = lax.broadcasted_iota(jnp.int32, (Z, 128), 1)
    row = lax.broadcasted_iota(jnp.int32, (Z, 128), 0)
    upper = lax.broadcasted_iota(jnp.int32, (Z, WIDTH), 0) >= Z // 2
    for x in range(X_LO):
        for core in range(CORE):
            spread = jnp.zeros((Z, 128), F32)
            for q in range(Q):
                pipe = (core + q) % 2
                low, high = (both_ref[p, q * X_LO + x].astype(F32) for p in (pipe, 1 - pipe))
                weights = jnp.where(upper, high, low)
                scale = (jnp.max(jnp.abs(weights), axis=-1, keepdims=True) + EPS_SCALE).astype(BF16).astype(F32)
                values = weights / scale
                for half in range(2):
                    rows_in_order[half, pl.ds(q, Z, stride=Q), :] = values[:, half * 128 : half * 128 + 128]
                spread = jnp.where(lane % Q == q, scale, spread)
            for half in range(2):
                values_ref[x, core, :, half * 128 : half * 128 + 128] = rows_in_order[half].astype(BF16)
            at = x * CORE + core
            scale_rows[at : at + 1, :] = jnp.sum(jnp.where(lane // Q == row, spread, 0.0), axis=0, keepdims=True)
    scales_ref[...] = scale_rows[...].astype(BF16)


def vmem(count):
    return [pl.BlockSpec(memory_space=pltpu.VMEM)] * count


def scalar():
    return pl.BlockSpec(memory_space=pltpu.SMEM)


def device(x_lo, pipe, z, y, x_hi):
    core = (pipe + x_hi + z // (Z // 2)) % 2
    return (((x_lo * CORE + core) * Z + z) * Y + y) * X_HI + x_hi


CHIPS = [(x_lo, z, y, x_hi) for y in range(Y) for x_hi in range(X_HI) for x_lo in range(X_LO) for z in range(Z)]
PAIRS = [[device(x, p, z, y, h) for p in range(CORE)] for x, z, y, h in CHIPS]
COLUMNS = [[device(x, p, z, y, h) for z in range(Z)] for p in range(CORE) for x, at, y, h in CHIPS if at == 0]
PLANES = [[device(x, p, z, y, h) for x, at, y, h in CHIPS if at == z] for p in range(CORE) for z in range(Z)]


def exchange(rows, groups):
    return lax.all_to_all(rows, "device", split_axis=0, concat_axis=0, axis_index_groups=groups, tiled=True)


def both_cores(rows):
    return lax.all_gather(rows, "device", axis=0, axis_index_groups=PAIRS, tiled=False)


def on_device(grads, master, moment, second):
    here = lax.axis_index("device").astype(jnp.int32)
    z_index = ((here >> 4) & 7)[None]
    pipe_index = (((here >> 7) ^ here ^ (here >> 6)) & 1)[None]
    half = jax.ShapeDtypeStruct((X_LO, Z * Q, WIDTH), BF16)
    send, own = pl.pallas_call(
        split_kernel,
        out_shape=(half, half),
        in_specs=[scalar(), scalar(), *vmem(1)],
        out_specs=vmem(2),
        compiler_params=SMALL,
    )(pipe_index, z_index, grads.reshape(X_LO, CORE, Z * Q, WIDTH))
    pair = pl.pallas_call(
        pair_sum_kernel,
        out_shape=jax.ShapeDtypeStruct((PEERS, Z, WIDTH), BF16),
        in_specs=[scalar(), *vmem(2)],
        out_specs=vmem(1)[0],
        scratch_shapes=[pltpu.VMEM((2, X_LO * Z * Q, 128), F32)],
        compiler_params=SMALL,
    )(pipe_index, own, both_cores(send))
    column = pl.pallas_call(
        plane_sum_kernel,
        out_shape=jax.ShapeDtypeStruct((Z, 16, WIDTH), BF16),
        in_specs=vmem(4),
        out_specs=vmem(1)[0],
        compiler_params=SMALL,
    )(exchange(pair, PLANES), master, moment, second)
    state = jax.ShapeDtypeStruct((1, WIDTH), F32)
    weights, mine = pl.pallas_call(
        update_kernel,
        out_shape=(jax.ShapeDtypeStruct((PEERS, Z, WIDTH), BF16), state),
        in_specs=[scalar(), *vmem(1)],
        out_specs=vmem(2),
        compiler_params=SMALL,
    )(z_index, exchange(column, COLUMNS))
    gathered = both_cores(exchange(weights, PLANES))
    values, scales, master_new, moment_new, second_new = pl.pallas_call(
        quantize_kernel,
        out_shape=(
            jax.ShapeDtypeStruct((X_LO, CORE, Z * Q, WIDTH), BF16),
            jax.ShapeDtypeStruct((X_LO * CORE, Z * Q), BF16),
            state,
            state,
            state,
        ),
        in_specs=vmem(5),
        out_specs=vmem(5),
        scratch_shapes=[pltpu.VMEM((2, Z * Q, 128), F32), pltpu.VMEM((X_LO * CORE, Z * Q), F32)],
        compiler_params=SMALL,
    )(gathered, mine, master, moment, second)
    return (master_new, moment_new, second_new, values.reshape(-1, WIDTH), scales.reshape(-1))


def solution(mesh):
    devices = Mesh(mesh.devices.reshape(-1), ("device",))
    rows = P("device", None)
    return jax.shard_map(
        on_device,
        mesh=devices,
        in_specs=(P("device", None, None), rows, rows, rows),
        out_specs=(rows, rows, rows, P(), P()),
        check_vma=False,
    )
```

```python
import jax
import jax.numpy as jnp
from jax import lax
from jax.experimental import pallas as pl
from jax.experimental.pallas import tpu as pltpu
from jax.sharding import Mesh
from jax.sharding import PartitionSpec as P

EPS_SCALE = 1e-05
BETA_ONE = 0.9
BETA_TWO = 0.95
LEARN_RATE = 0.02
DECAY_RATE = 0.1
EPS_ADAM = 1e-08
CORRECT_ONE = 1.0 - 0.9**10
CORRECT_TWO = 1.0 - 0.95**10

X_LO, CORE, Z, Y, X_HI = 4, 2, 8, 8, 2
Q = Y * X_HI
PEERS = X_LO * Q
WIDTH = 256
F32 = jnp.float32
BF16 = jnp.bfloat16
SMALL = pltpu.CompilerParams(vmem_limit_bytes=8 * 2**20)


def split_kernel(pipe_ref, z_ref, grads_ref, send_ref, own_ref):
    row = lax.broadcasted_iota(jnp.int32, (Z * Q, WIDTH), 0)
    swapped = (row // (Z * Q // 2) + pipe_ref[0]) % 2 == 1
    for x in range(X_LO):
        first, second = grads_ref[x, 0].astype(F32), grads_ref[x, 1].astype(F32)
        own_ref[x] = jnp.where(swapped, second, first).astype(BF16)
        send_ref[x] = jnp.where(swapped, first, second).astype(BF16)


def pair_sum_kernel(pipe_ref, own_ref, sent_ref, out_ref, total):
    other = 1 - pipe_ref[0]
    for x in range(X_LO):
        rows = pl.ds(x * Z * Q, Z * Q)
        both = own_ref[x].astype(F32) + sent_ref[other, x].astype(F32)
        for half in range(2):
            total[half, rows, :] = both[:, half * 128 : half * 128 + 128]
    for x in range(X_LO):
        for q in range(Q):
            for half in range(2):
                picked = total[half, pl.ds(x * Z * Q + q, Z, stride=Q), :]
                out_ref[q * X_LO + x, :, half * 128 : half * 128 + 128] = picked.astype(BF16)


def pieces(values, count):
    parts = []
    for _ in range(count):
        parts.append(values.astype(BF16).astype(F32))
        values = values - parts[-1]
    return parts


def plane_sum_kernel(got_ref, master_ref, moment_ref, second_ref, out_ref):
    lanes = [got_ref[p].astype(F32) for p in range(8)]
    for p in range(8, PEERS):
        lanes[p % 8] = lanes[p % 8] + got_ref[p].astype(F32)
    while len(lanes) > 1:
        lanes = [a + b for a, b in zip(lanes[::2], lanes[1::2])]
    parts = [*pieces(master_ref[...], 3), *pieces(moment_ref[...], 2), *pieces(second_ref[...], 2)]
    parts.append(jnp.zeros((1, WIDTH), F32))
    rows = jnp.concatenate([lanes[0], *parts], axis=0).astype(BF16)
    for p in range(Z):
        out_ref[p] = rows


def adamw(master, moment, second, summed):
    moment_new = BETA_ONE * moment + (1.0 - BETA_ONE) * summed
    second_new = BETA_TWO * second + (1.0 - BETA_TWO) * summed * summed
    update = moment_new / CORRECT_ONE / (jnp.sqrt(second_new / CORRECT_TWO) + EPS_ADAM)
    return master - LEARN_RATE * (update + DECAY_RATE * master), moment_new, second_new


def update_kernel(z_ref, got_ref, out_ref, mine_ref):
    got = [got_ref[p].astype(F32) for p in range(Z)]
    summed = got[0][0:8]
    for p in range(1, Z):
        summed = summed + got[p][0:8]
    row = lax.broadcasted_iota(jnp.int32, (Z, WIDTH), 0)

    def state(first, count):
        rows = jnp.zeros((Z, WIDTH), F32)
        for p in range(Z):
            value = got[p][first : first + 1]
            for k in range(1, count):
                value = value + got[p][first + k : first + k + 1]
            rows = jnp.where(row == p, value, rows)
        return rows

    sent = adamw(state(8, 3), state(11, 2), state(13, 2), summed)[0].astype(BF16)
    for p in range(PEERS):
        out_ref[p] = sent
    mine_ref[...] = jnp.sum(jnp.where(row == z_ref[0], summed, 0.0), axis=0, keepdims=True)


def quantize_kernel(
    both_ref, mine_ref, master_in, moment_in, second_in,
    values_ref, scales_ref, master_ref, moment_ref, second_ref, rows_in_order, scale_rows,
):
    own = adamw(master_in[...], moment_in[...], second_in[...], mine_ref[...])
    master_ref[...], moment_ref[...], second_ref[...] = own
    lane = lax.broadcasted_iota(jnp.int32, (Z, 128), 1)
    row = lax.broadcasted_iota(jnp.int32, (Z, 128), 0)
    upper = lax.broadcasted_iota(jnp.int32, (Z, WIDTH), 0) >= Z // 2
    for x in range(X_LO):
        for core in range(CORE):
            spread = jnp.zeros((Z, 128), F32)
            for q in range(Q):
                low, high = (both_ref[p, q * X_LO + x].astype(F32) for p in (core, 1 - core))
                weights = jnp.where(upper, high, low)
                scale = (jnp.max(jnp.abs(weights), axis=-1, keepdims=True) + EPS_SCALE).astype(BF16).astype(F32)
                values = weights / scale
                for half in range(2):
                    rows_in_order[half, pl.ds(q, Z, stride=Q), :] = values[:, half * 128 : half * 128 + 128]
                spread = jnp.where(lane % Q == q, scale, spread)
            for half in range(2):
                values_ref[x, core, :, half * 128 : half * 128 + 128] = rows_in_order[half].astype(BF16)
            at = x * CORE + core
            scale_rows[at : at + 1, :] = jnp.sum(jnp.where(lane // Q == row, spread, 0.0), axis=0, keepdims=True)
    scales_ref[...] = scale_rows[...].astype(BF16)


def vmem(count):
    return [pl.BlockSpec(memory_space=pltpu.VMEM)] * count


def scalar():
    return pl.BlockSpec(memory_space=pltpu.SMEM)


def device(x_lo, pipe, z, y, x_hi):
    core = (pipe + z // (Z // 2)) % 2
    return (((x_lo * CORE + core) * Z + z) * Y + y) * X_HI + x_hi


CHIPS = [(x_lo, z, y, x_hi) for y in range(Y) for x_hi in range(X_HI) for x_lo in range(X_LO) for z in range(Z)]
PAIRS = [[device(x, p, z, y, h) for p in range(CORE)] for x, z, y, h in CHIPS]
COLUMNS = [[device(x, p, z, y, h) for z in range(Z)] for p in range(CORE) for x, at, y, h in CHIPS if at == 0]
PLANES = [[device(x, p, z, y, h) for x, at, y, h in CHIPS if at == z] for p in range(CORE) for z in range(Z)]


def exchange(rows, groups):
    return lax.all_to_all(rows, "device", split_axis=0, concat_axis=0, axis_index_groups=groups, tiled=True)


def both_cores(rows):
    return lax.all_gather(rows, "device", axis=0, axis_index_groups=PAIRS, tiled=False)


def on_device(grads, master, moment, second):
    here = lax.axis_index("device").astype(jnp.int32)
    z_index = ((here >> 4) & 7)[None]
    pipe_index = (((here >> 7) ^ (here >> 6)) & 1)[None]
    half = jax.ShapeDtypeStruct((X_LO, Z * Q, WIDTH), BF16)
    send, own = pl.pallas_call(
        split_kernel,
        out_shape=(half, half),
        in_specs=[scalar(), scalar(), *vmem(1)],
        out_specs=vmem(2),
        compiler_params=SMALL,
    )(pipe_index, z_index, grads.reshape(X_LO, CORE, Z * Q, WIDTH))
    pair = pl.pallas_call(
        pair_sum_kernel,
        out_shape=jax.ShapeDtypeStruct((PEERS, Z, WIDTH), BF16),
        in_specs=[scalar(), *vmem(2)],
        out_specs=vmem(1)[0],
        scratch_shapes=[pltpu.VMEM((2, X_LO * Z * Q, 128), F32)],
        compiler_params=SMALL,
    )(pipe_index, own, both_cores(send))
    column = pl.pallas_call(
        plane_sum_kernel,
        out_shape=jax.ShapeDtypeStruct((Z, 16, WIDTH), BF16),
        in_specs=vmem(4),
        out_specs=vmem(1)[0],
        compiler_params=SMALL,
    )(exchange(pair, PLANES), master, moment, second)
    state = jax.ShapeDtypeStruct((1, WIDTH), F32)
    weights, mine = pl.pallas_call(
        update_kernel,
        out_shape=(jax.ShapeDtypeStruct((PEERS, Z, WIDTH), BF16), state),
        in_specs=[scalar(), *vmem(1)],
        out_specs=vmem(2),
        compiler_params=SMALL,
    )(z_index, exchange(column, COLUMNS))
    gathered = both_cores(exchange(weights, PLANES))
    values, scales, master_new, moment_new, second_new = pl.pallas_call(
        quantize_kernel,
        out_shape=(
            jax.ShapeDtypeStruct((X_LO, CORE, Z * Q, WIDTH), BF16),
            jax.ShapeDtypeStruct((X_LO * CORE, Z * Q), BF16),
            state,
            state,
            state,
        ),
        in_specs=vmem(5),
        out_specs=vmem(5),
        scratch_shapes=[pltpu.VMEM((2, Z * Q, 128), F32), pltpu.VMEM((X_LO * CORE, Z * Q), F32)],
        compiler_params=SMALL,
    )(gathered, mine, master, moment, second)
    return (master_new, moment_new, second_new, values.reshape(-1, WIDTH), scales.reshape(-1))


def solution(mesh):
    devices = Mesh(mesh.devices.reshape(-1), ("device",))
    rows = P("device", None)
    return jax.shard_map(
        on_device,
        mesh=devices,
        in_specs=(P("device", None, None), rows, rows, rows),
        out_specs=(rows, rows, rows, P(), P()),
        check_vma=False,
    )
```

```python
import jax
import jax.numpy as jnp
from jax import lax
from jax.experimental import pallas as pl
from jax.experimental.pallas import tpu as pltpu
from jax.sharding import Mesh
from jax.sharding import PartitionSpec as P

EPS_SCALE = 1e-05
BETA_ONE = 0.9
BETA_TWO = 0.95
LEARN_RATE = 0.02
DECAY_RATE = 0.1
EPS_ADAM = 1e-08
CORRECT_ONE = 1.0 - 0.9**10
CORRECT_TWO = 1.0 - 0.95**10

AXES = ("x_lo", "core", "z", "y", "x_hi")
SIZES = (4, 2, 8, 8, 2)
X_LO, CORE, Z, Y, X_HI = SIZES
PLANE = ("y", "x_hi", "x_lo")
Q = Y * X_HI
PEERS = X_LO * Q
WIDTH = 256
F32 = jnp.float32
BF16 = jnp.bfloat16
SMALL = pltpu.CompilerParams(vmem_limit_bytes=8 * 2**20)


def split_kernel(core_ref, z_ref, grads_ref, send_ref, own_ref, sems):
    core = core_ref[0]
    copies = [
        pltpu.make_async_copy(grads_ref.at[:, 1 - core], send_ref, sems.at[0]),
        pltpu.make_async_copy(grads_ref.at[:, core], own_ref, sems.at[1]),
    ]
    for copy in copies:
        copy.start()
    for copy in copies:
        copy.wait()


def pair_sum_kernel(core_ref, own_ref, sent_ref, out_ref, total):
    core = core_ref[0]
    for x in range(X_LO):
        rows = pl.ds(x * Z * Q, Z * Q)
        both = own_ref[x].astype(F32) + sent_ref[1 - core, x].astype(F32)
        for half in range(2):
            total[half, rows, :] = both[:, half * 128 : half * 128 + 128]
    for x in range(X_LO):
        for q in range(Q):
            for half in range(2):
                picked = total[half, pl.ds(x * Z * Q + q, Z, stride=Q), :]
                out_ref[q * X_LO + x, :, half * 128 : half * 128 + 128] = picked.astype(BF16)


def pieces(values, count):
    parts = []
    for _ in range(count):
        parts.append(values.astype(BF16).astype(F32))
        values = values - parts[-1]
    return parts


def plane_sum_kernel(got_ref, master_ref, moment_ref, second_ref, out_ref):
    lanes = [got_ref[p].astype(F32) for p in range(8)]
    for p in range(8, PEERS):
        lanes[p % 8] = lanes[p % 8] + got_ref[p].astype(F32)
    while len(lanes) > 1:
        lanes = [a + b for a, b in zip(lanes[::2], lanes[1::2])]
    parts = [*pieces(master_ref[...], 3), *pieces(moment_ref[...], 2), *pieces(second_ref[...], 2)]
    parts.append(jnp.zeros((1, WIDTH), F32))
    rows = jnp.concatenate([lanes[0], *parts], axis=0).astype(BF16)
    for p in range(Z):
        out_ref[p] = rows


def adamw(master, moment, second, summed):
    moment_new = BETA_ONE * moment + (1.0 - BETA_ONE) * summed
    second_new = BETA_TWO * second + (1.0 - BETA_TWO) * summed * summed
    update = moment_new / CORRECT_ONE / (jnp.sqrt(second_new / CORRECT_TWO) + EPS_ADAM)
    return master - LEARN_RATE * (update + DECAY_RATE * master), moment_new, second_new


def update_kernel(z_ref, got_ref, out_ref, mine_ref):
    got = [got_ref[p].astype(F32) for p in range(Z)]
    summed = got[0][0:8]
    for p in range(1, Z):
        summed = summed + got[p][0:8]
    row = lax.broadcasted_iota(jnp.int32, (Z, WIDTH), 0)

    def state(first, count):
        rows = jnp.zeros((Z, WIDTH), F32)
        for p in range(Z):
            value = got[p][first : first + 1]
            for k in range(1, count):
                value = value + got[p][first + k : first + k + 1]
            rows = jnp.where(row == p, value, rows)
        return rows

    sent = adamw(state(8, 3), state(11, 2), state(13, 2), summed)[0].astype(BF16)
    for p in range(PEERS):
        out_ref[p] = sent
    mine_ref[...] = jnp.sum(jnp.where(row == z_ref[0], summed, 0.0), axis=0, keepdims=True)


def quantize_kernel(
    both_ref, mine_ref, master_in, moment_in, second_in,
    values_ref, scales_ref, master_ref, moment_ref, second_ref, rows_in_order, scale_rows,
):
    x = pl.program_id(0)

    @pl.when(x == 0)
    def own_state():
        own = adamw(master_in[...], moment_in[...], second_in[...], mine_ref[...])
        master_ref[...], moment_ref[...], second_ref[...] = own

    lane = lax.broadcasted_iota(jnp.int32, (Z, 128), 1)
    row = lax.broadcasted_iota(jnp.int32, (Z, 128), 0)
    for core in range(CORE):
        spread = jnp.zeros((Z, 128), F32)
        for q in range(Q):
            weights = both_ref[core, q * X_LO + x].astype(F32)
            scale = (jnp.max(jnp.abs(weights), axis=-1, keepdims=True) + EPS_SCALE).astype(BF16).astype(F32)
            values = weights / scale
            for half in range(2):
                rows_in_order[half, pl.ds(q, Z, stride=Q), :] = values[:, half * 128 : half * 128 + 128]
            spread = jnp.where(lane % Q == q, scale, spread)
        for half in range(2):
            values_ref[0, core, :, half * 128 : half * 128 + 128] = rows_in_order[half].astype(BF16)
        scale_rows[pl.ds(x * CORE + core, 1), :] = jnp.sum(
            jnp.where(lane // Q == row, spread, 0.0), axis=0, keepdims=True
        )

    @pl.when(x == X_LO - 1)
    def all_scales():
        scales_ref[...] = scale_rows[...].astype(BF16)


def vmem(count):
    return [pl.BlockSpec(memory_space=pltpu.VMEM)] * count


def scalar():
    return pl.BlockSpec(memory_space=pltpu.SMEM)


def exchange(rows, axis):
    return lax.all_to_all(rows, axis, split_axis=0, concat_axis=0, tiled=True)


def both_cores(rows):
    return lax.all_gather(rows, "core", axis=0, tiled=False)


def on_device(grads, master, moment, second):
    core_index = lax.axis_index("core").astype(jnp.int32)[None]
    z_index = lax.axis_index("z").astype(jnp.int32)[None]
    half = jax.ShapeDtypeStruct((X_LO, Z * Q, WIDTH), BF16)
    send, own = pl.pallas_call(
        split_kernel,
        out_shape=(half, half),
        in_specs=[scalar(), scalar(), pl.BlockSpec(memory_space=pltpu.HBM)],
        out_specs=vmem(2),
        scratch_shapes=[pltpu.SemaphoreType.DMA((2,))],
        compiler_params=SMALL,
    )(core_index, z_index, grads.reshape(X_LO, CORE, Z * Q, WIDTH))
    pair = pl.pallas_call(
        pair_sum_kernel,
        out_shape=jax.ShapeDtypeStruct((PEERS, Z, WIDTH), BF16),
        in_specs=[scalar(), *vmem(2)],
        out_specs=vmem(1)[0],
        scratch_shapes=[pltpu.VMEM((2, X_LO * Z * Q, 128), F32)],
        compiler_params=SMALL,
    )(core_index, own, both_cores(send))
    column = pl.pallas_call(
        plane_sum_kernel,
        out_shape=jax.ShapeDtypeStruct((Z, 16, WIDTH), BF16),
        in_specs=vmem(4),
        out_specs=vmem(1)[0],
        compiler_params=SMALL,
    )(exchange(pair, PLANE), master, moment, second)
    state = jax.ShapeDtypeStruct((1, WIDTH), F32)
    weights, mine = pl.pallas_call(
        update_kernel,
        out_shape=(jax.ShapeDtypeStruct((PEERS, Z, WIDTH), BF16), state),
        in_specs=[scalar(), *vmem(1)],
        out_specs=vmem(2),
        compiler_params=SMALL,
    )(z_index, exchange(column, "z"))
    gathered = both_cores(exchange(weights, PLANE))
    values, scales, master_new, moment_new, second_new = pl.pallas_call(
        quantize_kernel,
        out_shape=(
            jax.ShapeDtypeStruct((X_LO, CORE, Z * Q, WIDTH), BF16),
            jax.ShapeDtypeStruct((X_LO * CORE, Z * Q), BF16),
            state,
            state,
            state,
        ),
        grid=(X_LO,),
        in_specs=vmem(5),
        out_specs=[pl.BlockSpec((1, CORE, Z * Q, WIDTH), lambda x: (x, 0, 0, 0)), *vmem(4)],
        scratch_shapes=[pltpu.VMEM((2, Z * Q, 128), F32), pltpu.VMEM((X_LO * CORE, Z * Q), F32)],
        compiler_params=SMALL,
    )(gathered, mine, master, moment, second)
    return (master_new, moment_new, second_new, values.reshape(-1, WIDTH), scales.reshape(-1))


def solution(mesh):
    devices = Mesh(mesh.devices.reshape(SIZES), AXES)
    rows = P(AXES, None)
    return jax.shard_map(
        on_device,
        mesh=devices,
        in_specs=(P(AXES, None, None), rows, rows, rows),
        out_specs=(rows, rows, rows, P(), P()),
        check_vma=False,
    )
```

```python
import jax
import jax.numpy as jnp
from jax import lax
from jax.experimental import pallas as pl
from jax.experimental.pallas import tpu as pltpu
from jax.sharding import Mesh
from jax.sharding import PartitionSpec as P

EPS_SCALE = 1e-05
BETA_ONE = 0.9
BETA_TWO = 0.95
LEARN_RATE = 0.02
DECAY_RATE = 0.1
EPS_ADAM = 1e-08
CORRECT_ONE = 1.0 - 0.9**10
CORRECT_TWO = 1.0 - 0.95**10

X_LO, CORE, Z, Y, X_HI = 4, 2, 8, 8, 2
Q = Y * X_HI
PEERS = X_LO * Q
WIDTH = 256
F32 = jnp.float32
BF16 = jnp.bfloat16


def peer(core, x, q):
    y, x_hi = q // X_HI, q % X_HI
    return (x_hi * X_LO + x) * Y + y if core else q * X_LO + x


SMALL = pltpu.CompilerParams(vmem_limit_bytes=8 * 2**20)


def split_kernel(core_ref, z_ref, grads_ref, send_ref, own_ref, sems):
    core = core_ref[0]
    copies = [
        pltpu.make_async_copy(grads_ref.at[:, 1 - core], send_ref, sems.at[0]),
        pltpu.make_async_copy(grads_ref.at[:, core], own_ref, sems.at[1]),
    ]
    for copy in copies:
        copy.start()
    for copy in copies:
        copy.wait()


def pair_sum_kernel(core_ref, own_ref, sent_ref, out_ref, total):
    core = core_ref[0]
    for x in range(X_LO):
        rows = pl.ds(x * Z * Q, Z * Q)
        both = own_ref[x].astype(F32) + sent_ref[1 - core, x].astype(F32)
        for half in range(2):
            total[half, rows, :] = both[:, half * 128 : half * 128 + 128]
    for x in range(X_LO):
        for q in range(Q):
            for half in range(2):
                picked = total[half, pl.ds(x * Z * Q + q, Z, stride=Q), :]
                at = peer(0, x, q) + core * (peer(1, x, q) - peer(0, x, q))
                out_ref[at, :, half * 128 : half * 128 + 128] = picked.astype(BF16)


def pieces(values, count):
    parts = []
    for _ in range(count):
        parts.append(values.astype(BF16).astype(F32))
        values = values - parts[-1]
    return parts


def plane_sum_kernel(got_ref, master_ref, moment_ref, second_ref, out_ref):
    lanes = [got_ref[p].astype(F32) for p in range(8)]
    for p in range(8, PEERS):
        lanes[p % 8] = lanes[p % 8] + got_ref[p].astype(F32)
    while len(lanes) > 1:
        lanes = [a + b for a, b in zip(lanes[::2], lanes[1::2])]
    parts = [*pieces(master_ref[...], 3), *pieces(moment_ref[...], 2), *pieces(second_ref[...], 2)]
    parts.append(jnp.zeros((1, WIDTH), F32))
    rows = jnp.concatenate([lanes[0], *parts], axis=0).astype(BF16)
    for p in range(Z):
        out_ref[p] = rows


def adamw(master, moment, second, summed):
    moment_new = BETA_ONE * moment + (1.0 - BETA_ONE) * summed
    second_new = BETA_TWO * second + (1.0 - BETA_TWO) * summed * summed
    update = moment_new / CORRECT_ONE / (jnp.sqrt(second_new / CORRECT_TWO) + EPS_ADAM)
    return master - LEARN_RATE * (update + DECAY_RATE * master), moment_new, second_new


def update_kernel(z_ref, got_ref, out_ref, mine_ref):
    got = [got_ref[p].astype(F32) for p in range(Z)]
    summed = got[0][0:8]
    for p in range(1, Z):
        summed = summed + got[p][0:8]
    row = lax.broadcasted_iota(jnp.int32, (Z, WIDTH), 0)

    def state(first, count):
        rows = jnp.zeros((Z, WIDTH), F32)
        for p in range(Z):
            value = got[p][first : first + 1]
            for k in range(1, count):
                value = value + got[p][first + k : first + k + 1]
            rows = jnp.where(row == p, value, rows)
        return rows

    sent = adamw(state(8, 3), state(11, 2), state(13, 2), summed)[0].astype(BF16)
    for p in range(PEERS):
        out_ref[p] = sent
    mine_ref[...] = jnp.sum(jnp.where(row == z_ref[0], summed, 0.0), axis=0, keepdims=True)


def quantize_kernel(
    both_ref, mine_ref, master_in, moment_in, second_in,
    values_ref, scales_ref, master_ref, moment_ref, second_ref, rows_in_order, scale_rows,
):
    own = adamw(master_in[...], moment_in[...], second_in[...], mine_ref[...])
    master_ref[...], moment_ref[...], second_ref[...] = own
    lane = lax.broadcasted_iota(jnp.int32, (Z, 128), 1)
    row = lax.broadcasted_iota(jnp.int32, (Z, 128), 0)
    for x in range(X_LO):
        for core in range(CORE):
            spread = jnp.zeros((Z, 128), F32)
            for q in range(Q):
                weights = both_ref[core, peer(core, x, q)].astype(F32)
                scale = (jnp.max(jnp.abs(weights), axis=-1, keepdims=True) + EPS_SCALE).astype(BF16).astype(F32)
                values = weights / scale
                for half in range(2):
                    rows_in_order[half, pl.ds(q, Z, stride=Q), :] = values[:, half * 128 : half * 128 + 128]
                spread = jnp.where(lane % Q == q, scale, spread)
            for half in range(2):
                values_ref[x, core, :, half * 128 : half * 128 + 128] = rows_in_order[half].astype(BF16)
            at = x * CORE + core
            scale_rows[at : at + 1, :] = jnp.sum(jnp.where(lane // Q == row, spread, 0.0), axis=0, keepdims=True)
    scales_ref[...] = scale_rows[...].astype(BF16)


def vmem(count):
    return [pl.BlockSpec(memory_space=pltpu.VMEM)] * count


def scalar():
    return pl.BlockSpec(memory_space=pltpu.SMEM)


def device(x_lo, core, z, q):
    return ((x_lo * CORE + core) * Z + z) * Q + q


def plane(core, z):
    places = sorted((peer(core, x, q), x, q) for x in range(X_LO) for q in range(Q))
    return [device(x, core, z, q) for _, x, q in places]


PLANES = [plane(core, z) for core in range(CORE) for z in range(Z)]
COLUMNS = [[device(x, core, z, q) for z in range(Z)] for x in range(X_LO) for core in range(CORE) for q in range(Q)]
PAIRS = [[device(x, core, z, q) for core in range(CORE)] for x in range(X_LO) for z in range(Z) for q in range(Q)]


def exchange(rows, groups):
    return lax.all_to_all(rows, "device", split_axis=0, concat_axis=0, axis_index_groups=groups, tiled=True)


def both_cores(rows):
    return lax.all_gather(rows, "device", axis=0, axis_index_groups=PAIRS, tiled=False)


def on_device(grads, master, moment, second):
    here = lax.axis_index("device").astype(jnp.int32)
    core_index = ((here >> 7) & 1)[None]
    z_index = ((here >> 4) & 7)[None]
    half = jax.ShapeDtypeStruct((X_LO, Z * Q, WIDTH), BF16)
    send, own = pl.pallas_call(
        split_kernel,
        out_shape=(half, half),
        in_specs=[scalar(), scalar(), pl.BlockSpec(memory_space=pltpu.HBM)],
        out_specs=vmem(2),
        scratch_shapes=[pltpu.SemaphoreType.DMA((2,))],
        compiler_params=SMALL,
    )(core_index, z_index, grads.reshape(X_LO, CORE, Z * Q, WIDTH))
    pair = pl.pallas_call(
        pair_sum_kernel,
        out_shape=jax.ShapeDtypeStruct((PEERS, Z, WIDTH), BF16),
        in_specs=[scalar(), *vmem(2)],
        out_specs=vmem(1)[0],
        scratch_shapes=[pltpu.VMEM((2, X_LO * Z * Q, 128), F32)],
        compiler_params=SMALL,
    )(core_index, own, both_cores(send))
    column = pl.pallas_call(
        plane_sum_kernel,
        out_shape=jax.ShapeDtypeStruct((Z, 16, WIDTH), BF16),
        in_specs=vmem(4),
        out_specs=vmem(1)[0],
        compiler_params=SMALL,
    )(exchange(pair, PLANES), master, moment, second)
    state = jax.ShapeDtypeStruct((1, WIDTH), F32)
    weights, mine = pl.pallas_call(
        update_kernel,
        out_shape=(jax.ShapeDtypeStruct((PEERS, Z, WIDTH), BF16), state),
        in_specs=[scalar(), *vmem(1)],
        out_specs=vmem(2),
        compiler_params=SMALL,
    )(z_index, exchange(column, COLUMNS))
    gathered = both_cores(exchange(weights, PLANES))
    values, scales, master_new, moment_new, second_new = pl.pallas_call(
        quantize_kernel,
        out_shape=(
            jax.ShapeDtypeStruct((X_LO, CORE, Z * Q, WIDTH), BF16),
            jax.ShapeDtypeStruct((X_LO * CORE, Z * Q), BF16),
            state,
            state,
            state,
        ),
        in_specs=vmem(5),
        out_specs=vmem(5),
        scratch_shapes=[pltpu.VMEM((2, Z * Q, 128), F32), pltpu.VMEM((X_LO * CORE, Z * Q), F32)],
        compiler_params=SMALL,
    )(gathered, mine, master, moment, second)
    return (master_new, moment_new, second_new, values.reshape(-1, WIDTH), scales.reshape(-1))


def solution(mesh):
    devices = Mesh(mesh.devices.reshape(-1), ("device",))
    rows = P("device", None)
    return jax.shard_map(
        on_device,
        mesh=devices,
        in_specs=(P("device", None, None), rows, rows, rows),
        out_specs=(rows, rows, rows, P(), P()),
        check_vma=False,
    )
```
